32 devices in a mesh: groups: 2 (over y), seq: 8 (over z, core), head: 2 (over x).
Axes of the slice: x: 2, y: 2, z: 4, core: 2. Of those that a mesh axis runs over, the one named last changes fastest.
Arguments:
- query_rows: bfloat16 [4096, 1024], P(('groups', 'seq'), 'head'), parts along dimension 0, may hold values from -8 to 8
- key_rows: bfloat16 [4096, 1024], P(('groups', 'seq'), 'head'), parts along dimension 0, may hold values from -8 to 8
- value_rows: bfloat16 [4096, 1024], P(('groups', 'seq'), 'head'), parts along dimension 0, may hold values from -6 to 6
- grad_output: bfloat16 [4096, 1024], P(('groups', 'seq'), 'head'), parts along dimension 0, may hold values from -6 to 6
- dilation_offsets: int32 [1, 8], P(None, 'head'), may hold values from 0 to 0, as said below
Outputs:
- attended: bfloat16 [4096, 1024], P(('groups', 'seq'), 'head'), parts along dimension 0
- query_grad: bfloat16 [4096, 1024], P(('groups', 'seq'), 'head'), parts along dimension 0
- key_grad: bfloat16 [4096, 1024], P(('groups', 'seq'), 'head'), parts along dimension 0
- value_grad: bfloat16 [4096, 1024], P(('groups', 'seq'), 'head'), parts along dimension 0
The draws below stay inside these ranges and needn't reach their ends.
There are 2 independent parts, one for each index of `groups`. The reference program is written for one: setup_inputs(seed, part) draws one part's arguments, and reference() takes and returns one part's arrays. A program takes and returns all parts, laid end to end along the dimension named above; an argument that names none is the same for every part. Nothing has to cross between parts.
Inputs may be any that keep to these rules, and one draw needn't show every extreme that they name: `dilation_offsets`: row l (counting from 0) holds for each head a number from 0 to 2^l - 1.
All inputs are finite; a program needn't handle non-finite values.
Results may differ from the reference program's by a relative error of at most 0.01.
Values may be sent and summed in bfloat16 or wider, within the bound.
No kernel may reach another device: no remote copies, remote signals or barrier semaphores. Data moves between devices by JAX's collectives and lax.ppermute only.
A program may use at most 128 MiB of HBM per device.

```python
import jax
import jax.numpy as jnp
from jax import lax

HEADS = 8
HD = 128
SEG = 2048
TOKENS = 2048
SPAN = 1
LEVELS = 1


def paired_fields(key):
    shape_all = (TOKENS, HEADS * HD)
    query_base = 1.4 * jax.random.truncated_normal(jax.random.fold_in(key, 11), -5.7, 5.7, shape_all, jnp.float32)
    key_base = 1.4 * jax.random.truncated_normal(jax.random.fold_in(key, 12), -5.7, 5.7, shape_all, jnp.float32)
    return (query_base, key_base)


def draw_query_rows(key, part):
    return paired_fields(key)[0].astype(jnp.bfloat16)


def draw_key_rows(key, part):
    return paired_fields(key)[1].astype(jnp.bfloat16)


def draw_dilation_offsets(key, part):
    drawn_values = jax.random.randint(jax.random.fold_in(key, 21), (LEVELS, HEADS), 0, SPAN, dtype=jnp.int32)
    moduli = 2 ** jnp.arange(LEVELS, dtype=jnp.int32)
    return drawn_values % moduli[:, None]


def levels(stream_key, extent, shards, low, high):
    factor_of = 1.0
    for axis_at, parts in shards:
        steps = jax.random.uniform(jax.random.fold_in(jax.random.fold_in(stream_key, 6), axis_at), (parts,), jnp.float32, low / len(shards), high / len(shards))
        factor_of = factor_of * jnp.repeat(jnp.exp(steps), extent[axis_at] // parts).reshape((-1,) + (1,) * (len(extent) - 1 - axis_at))
    return factor_of


def bell_draw(rng, extent, scale, bound, cuts=(), kind=jnp.bfloat16):
    values = scale * jax.random.normal(rng, extent, jnp.float32)
    if cuts:
        values = values * levels(rng, extent, cuts, -0.22, 0.18)
    return jnp.clip(values, -bound, bound).astype(kind)


def setup_inputs(seed: int = 0, part: int = 0) -> dict:
    streams_of = jax.random.split(jax.random.key(seed), 6)
    part_keys = jax.random.split(jax.random.fold_in(streams_of[5], part), 6)
    return {
        "query_rows": draw_query_rows(jax.random.fold_in(jax.random.fold_in(streams_of[5], part), 71), part),
        "key_rows": draw_key_rows(jax.random.fold_in(jax.random.fold_in(streams_of[5], part), 71), part),
        "value_rows": bell_draw(part_keys[2], (TOKENS, HEADS * HD), 1.0, 6.0, ((0, 8), (1, 2))),
        "grad_output": bell_draw(part_keys[3], (TOKENS, HEADS * HD), 1.0, 6.0, ((0, 8), (1, 2))),
        "dilation_offsets": draw_dilation_offsets(jax.random.fold_in(streams_of[5], 71), part),
    }


def select_rows(values, row_mask):
    stride = row_mask.shape[0]
    shaped = values.reshape((values.shape[0] // stride, stride) + values.shape[1:])
    mask_wide = row_mask.reshape(row_mask.shape + (1,) * (values.ndim - 2))
    return jnp.sum(jnp.where(mask_wide, shaped, jnp.zeros((), values.dtype)), axis=1)


def spread_rows(values, row_mask):
    stride = row_mask.shape[0]
    mask_wide = row_mask.reshape(row_mask.shape + (1,) * (values.ndim - 2))
    spread = jnp.where(mask_wide, values[:, None], jnp.zeros((), values.dtype))
    return spread.reshape((values.shape[0] * stride,) + values.shape[1:])


def forward_segment(operands):
    query_seg, key_seg, value_seg = operands
    score_scale = HD ** -0.5
    scores = jnp.einsum("nhd,khd->hnk", query_seg.astype(jnp.float32), key_seg.astype(jnp.float32)) * score_scale
    row_peak = jnp.max(scores, axis=2, keepdims=True)
    row_sums = jnp.sum(jnp.exp(scores - row_peak), axis=2, keepdims=True)
    level_lse = row_peak + jnp.log(row_sums)
    level_probs = jnp.exp(scores - level_lse).astype(jnp.bfloat16)
    partial_value = jnp.einsum("hnk,khd->nhd", level_probs.astype(jnp.float32), value_seg.astype(jnp.float32))
    return partial_value, jnp.transpose(level_lse[:, :, 0])


def backward_segment(operands):
    query_seg, key_seg, value_seg, grad_seg, total_seg, delta_seg = operands
    score_scale = HD ** -0.5
    scores = jnp.einsum("nhd,khd->hnk", query_seg.astype(jnp.float32), key_seg.astype(jnp.float32)) * score_scale
    glob = jnp.exp(scores - jnp.transpose(total_seg)[:, :, None])
    glob_low = glob.astype(jnp.bfloat16)
    value_part = jnp.einsum("hnk,nhd->khd", glob_low.astype(jnp.float32), grad_seg.astype(jnp.float32))
    dprob = jnp.einsum("nhd,khd->hnk", grad_seg.astype(jnp.float32), value_seg.astype(jnp.float32))
    dscore = (glob * (dprob - jnp.transpose(delta_seg)[:, :, None])).astype(jnp.bfloat16)
    query_part = jnp.einsum("hnk,khd->nhd", dscore.astype(jnp.float32), key_seg.astype(jnp.float32)) * score_scale
    key_part = jnp.einsum("hnk,nhd->khd", dscore.astype(jnp.float32), query_seg.astype(jnp.float32)) * score_scale
    return query_part, key_part, value_part


def reference(query_rows, key_rows, value_rows, grad_output, dilation_offsets):
    total_rows = query_rows.shape[0]
    head_count = query_rows.shape[1] // HD
    level_count = dilation_offsets.shape[0]
    query_three = query_rows.reshape(total_rows, head_count, HD)
    key_three = key_rows.reshape(total_rows, head_count, HD)
    value_three = value_rows.reshape(total_rows, head_count, HD)
    grad_three = grad_output.reshape(total_rows, head_count, HD)
    level_masks = []
    full_masks = []
    segments = []
    out_parts = []
    lse_full = []
    for level_no in range(level_count):
        stride = 2 ** level_no
        row_mask = lax.broadcasted_iota(jnp.int32, (stride, head_count), 0) == dilation_offsets[level_no][None, :]
        full_mask = (lax.broadcasted_iota(jnp.int32, (total_rows, head_count), 0) % stride) == dilation_offsets[level_no][None, :]
        level_masks.append(row_mask)
        full_masks.append(full_mask)
        query_seg = select_rows(query_three, row_mask).reshape(-1, SEG, head_count, HD)
        key_seg = select_rows(key_three, row_mask).reshape(-1, SEG, head_count, HD)
        value_seg = select_rows(value_three, row_mask).reshape(-1, SEG, head_count, HD)
        segments.append((query_seg, key_seg, value_seg))
        partial_value, level_lse = lax.map(forward_segment, (query_seg, key_seg, value_seg))
        out_parts.append(spread_rows(partial_value.reshape(-1, head_count, HD), row_mask))
        lse_full.append(spread_rows(level_lse.reshape(-1, head_count), row_mask))
    row_peak = lse_full[0]
    for level_no in range(1, level_count):
        row_peak = jnp.maximum(row_peak, jnp.where(full_masks[level_no], lse_full[level_no], lse_full[0]))
    exp_total = jnp.zeros((total_rows, head_count), jnp.float32)
    for level_no in range(level_count):
        exp_total = exp_total + jnp.where(full_masks[level_no], jnp.exp(lse_full[level_no] - row_peak), jnp.float32(0.0))
    total_lse = row_peak + jnp.log(exp_total)
    combined = jnp.zeros((total_rows, head_count, HD), jnp.float32)
    for level_no in range(level_count):
        weight = jnp.exp(lse_full[level_no] - total_lse)
        combined = combined + jnp.where(full_masks[level_no][:, :, None], weight[:, :, None] * out_parts[level_no], jnp.float32(0.0))
    attended = combined.astype(jnp.bfloat16)
    delta = jnp.sum(attended.astype(jnp.float32) * grad_three.astype(jnp.float32), axis=2)
    query_acc = jnp.zeros((total_rows, head_count, HD), jnp.float32)
    key_acc = jnp.zeros((total_rows, head_count, HD), jnp.float32)
    value_acc = jnp.zeros((total_rows, head_count, HD), jnp.float32)
    for level_no in range(level_count):
        row_mask = level_masks[level_no]
        query_seg, key_seg, value_seg = segments[level_no]
        grad_seg = select_rows(grad_three, row_mask).reshape(-1, SEG, head_count, HD)
        total_seg = select_rows(total_lse, row_mask).reshape(-1, SEG, head_count)
        delta_seg = select_rows(delta, row_mask).reshape(-1, SEG, head_count)
        query_part, key_part, value_part = lax.map(backward_segment, (query_seg, key_seg, value_seg, grad_seg, total_seg, delta_seg))
        query_acc = query_acc + spread_rows(query_part.reshape(-1, head_count, HD), row_mask)
        key_acc = key_acc + spread_rows(key_part.reshape(-1, head_count, HD), row_mask)
        value_acc = value_acc + spread_rows(value_part.reshape(-1, head_count, HD), row_mask)
    flat = (total_rows, head_count * HD)
    return (attended.reshape(flat), query_acc.astype(jnp.bfloat16).reshape(flat), key_acc.astype(jnp.bfloat16).reshape(flat), value_acc.astype(jnp.bfloat16).reshape(flat))
```

```python
import functools

import jax
import jax.numpy as jnp
from jax import lax
from jax.experimental import pallas as pl
from jax.experimental.pallas import tpu as pltpu
from jax.sharding import PartitionSpec as P

HD = 128
SEG = 2048


def shortened(array):

    def short(part):
        return part.astype(jnp.bfloat16) if part.dtype == jnp.float32 else part

    return jax.tree.map(short, array)


def from_partner(array, axis, stride):
    return lax.ppermute(array, axis, [(i, i ^ 1 << stride) for i in range(lax.axis_size(axis))])


def pick_rows(values, row_mask):
    stride = row_mask.shape[0]
    shaped = values.reshape((values.shape[0] // stride, stride) + values.shape[1:])
    mask_wide = row_mask.reshape(row_mask.shape + (1,) * (values.ndim - 2))
    return jnp.sum(jnp.where(mask_wide, shaped, jnp.zeros((), values.dtype)), axis=1)


def place_rows(values, row_mask):
    stride = row_mask.shape[0]
    mask_wide = row_mask.reshape(row_mask.shape + (1,) * (values.ndim - 2))
    spread = jnp.where(mask_wide, values[:, None], jnp.zeros((), values.dtype))
    return spread.reshape((values.shape[0] * stride,) + values.shape[1:])


def upper_of(seq_index, bit_number):
    return seq_index // 2**bit_number % 2 == 1


def widen_apart(buffers, bit_totals, seq_index):
    widened = []
    for buffer, bit_total in zip(buffers, bit_totals):
        for bit_number in range(bit_total):
            partner = jax.tree.map(
                lambda part, own: part.astype(own.dtype),
                from_partner(shortened(buffer), "seq", bit_number),
                buffer,
            )
            upper_side = upper_of(seq_index, bit_number)
            buffer = jnp.where(
                upper_side,
                jnp.concatenate([partner, buffer], 0),
                jnp.concatenate([buffer, partner], 0),
            )
        widened.append(buffer)
    return widened


def narrow_apart(buffers, bit_totals, seq_index):
    narrowed = []
    for buffer, bit_total in zip(buffers, bit_totals):
        for bit_number in reversed(range(bit_total)):
            half_rows = buffer.shape[0] // 2
            lower_half = buffer[:half_rows]
            upper_half = buffer[half_rows:]
            upper_side = upper_of(seq_index, bit_number)
            outgoing = jnp.where(upper_side, lower_half, upper_half)
            kept_half = jnp.where(upper_side, upper_half, lower_half)
            buffer = kept_half + from_partner(outgoing, "seq", bit_number)
        narrowed.append(buffer)
    return narrowed


def split_keys(gathered, head_count):
    width = head_count * HD
    key_all = gathered[:, :width].reshape(-1, head_count, HD)
    value_all = gathered[:, width : 2 * width].reshape(-1, head_count, HD)
    return (key_all, value_all)


def forward_level(query_part, gathered, head_count):
    score_scale = HD ** (-0.5)
    key_all, value_all = split_keys(gathered, head_count)
    scores = (
        jnp.einsum("nhd,khd->hnk", query_part, key_all, preferred_element_type=jnp.float32)
        * score_scale
    )
    row_peak = jnp.max(scores, axis=2, keepdims=True)
    row_sums = jnp.sum(jnp.exp(scores - row_peak), axis=2, keepdims=True)
    level_lse = row_peak + jnp.log(row_sums)
    level_probs = jnp.exp(scores - level_lse).astype(jnp.bfloat16)
    partial_value = jnp.einsum(
        "hnk,khd->nhd", level_probs, value_all, preferred_element_type=jnp.float32
    )
    return (partial_value, jnp.transpose(level_lse[:, :, 0]))


def backward_level(query_part, grad_part, total_part, delta_part, gathered, head_count):
    score_scale = HD ** (-0.5)
    key_all, value_all = split_keys(gathered, head_count)
    scores = (
        jnp.einsum("nhd,khd->hnk", query_part, key_all, preferred_element_type=jnp.float32)
        * score_scale
    )
    glob = jnp.exp(scores - jnp.transpose(total_part)[:, :, None])
    glob_low = glob.astype(jnp.bfloat16)
    value_part = jnp.einsum("hnk,nhd->khd", glob_low, grad_part, preferred_element_type=jnp.float32)
    dprob = jnp.einsum("nhd,khd->hnk", grad_part, value_all, preferred_element_type=jnp.float32)
    dscore = (glob * (dprob - jnp.transpose(delta_part)[:, :, None])).astype(jnp.bfloat16)
    query_part_grad = (
        jnp.einsum("hnk,khd->nhd", dscore, key_all, preferred_element_type=jnp.float32)
        * score_scale
    )
    key_part = (
        jnp.einsum("hnk,nhd->khd", dscore, query_part, preferred_element_type=jnp.float32)
        * score_scale
    )
    key_count = key_part.shape[0]
    grad_term = jnp.concatenate(
        [key_part.reshape(key_count, -1), value_part.reshape(key_count, -1)], axis=1
    )
    return (query_part_grad, grad_term)


def shards_levels(query_rows, key_rows, value_rows, grad_output, dilation_offsets):
    row_count = query_rows.shape[0]
    head_count = query_rows.shape[1] // HD
    level_count = dilation_offsets.shape[0]
    seq_index = lax.axis_index("seq")
    seq_width = lax.axis_size("seq")
    query_three = query_rows.reshape(row_count, head_count, HD)
    key_three = key_rows.reshape(row_count, head_count, HD)
    value_three = value_rows.reshape(row_count, head_count, HD)
    grad_three = grad_output.reshape(row_count, head_count, HD)
    level_masks = []
    full_masks = []
    query_parts = []
    kept_pieces = []
    segment_bits = []
    for level_no in range(level_count):
        stride = 2**level_no
        row_mask = (
            lax.broadcasted_iota(jnp.int32, (stride, head_count), 0)
            == dilation_offsets[level_no][None, :]
        )
        full_mask = (
            lax.broadcasted_iota(jnp.int32, (row_count, head_count), 0) % stride
            == dilation_offsets[level_no][None, :]
        )
        level_masks.append(row_mask)
        full_masks.append(full_mask)
        query_parts.append(pick_rows(query_three, row_mask))
        key_three_part = pick_rows(key_three, row_mask)
        value_three_part = pick_rows(value_three, row_mask)
        piece = jnp.concatenate(
            [
                key_three_part.reshape(row_count // stride, -1),
                value_three_part.reshape(row_count // stride, -1),
            ],
            axis=1,
        )
        kept_pieces.append(piece)
        segment_bits.append(
            min((SEG * stride // row_count).bit_length() - 1, seq_width.bit_length() - 1)
        )
    paired = list(range(level_count - 1))
    paired_bits = [segment_bits[member] for member in paired]
    widened = widen_apart([kept_pieces[member] for member in paired], paired_bits, seq_index)
    gathered = list(kept_pieces)
    for member, buffer in zip(paired, widened):
        gathered[member] = buffer
    gathered[level_count - 1] = lax.all_gather(
        kept_pieces[level_count - 1], "seq", axis=0, tiled=True
    )
    out_parts = []
    lse_full = []
    for level_no in range(level_count):
        partial_value, level_lse = forward_level(
            query_parts[level_no], gathered[level_no], head_count
        )
        out_parts.append(place_rows(partial_value, level_masks[level_no]))
        lse_full.append(place_rows(level_lse, level_masks[level_no]))
    row_peak = lse_full[0]
    for level_no in range(1, level_count):
        row_peak = jnp.maximum(
            row_peak, jnp.where(full_masks[level_no], lse_full[level_no], lse_full[0])
        )
    exp_total = jnp.zeros((row_count, head_count), jnp.float32)
    for level_no in range(level_count):
        exp_total = exp_total + jnp.where(
            full_masks[level_no], jnp.exp(lse_full[level_no] - row_peak), jnp.float32(0.0)
        )
    total_lse = row_peak + jnp.log(exp_total)
    combined = jnp.zeros((row_count, head_count, HD), jnp.float32)
    for level_no in range(level_count):
        weight = jnp.exp(lse_full[level_no] - total_lse)
        combined = combined + jnp.where(
            full_masks[level_no][:, :, None],
            weight[:, :, None] * out_parts[level_no],
            jnp.float32(0.0),
        )
    attended = combined.astype(jnp.bfloat16)
    delta = jnp.sum(attended.astype(jnp.float32) * grad_three.astype(jnp.float32), axis=2)
    query_acc = jnp.zeros((row_count, head_count, HD), jnp.float32)
    grad_terms = []
    for level_no in range(level_count):
        row_mask = level_masks[level_no]
        grad_part = pick_rows(grad_three, row_mask)
        total_part = pick_rows(total_lse, row_mask)
        delta_part = pick_rows(delta, row_mask)
        query_part_grad, grad_term = backward_level(
            query_parts[level_no], grad_part, total_part, delta_part, gathered[level_no], head_count
        )
        query_acc = query_acc + place_rows(query_part_grad, row_mask)
        grad_terms.append(grad_term)
    narrowed = narrow_apart([grad_terms[member] for member in paired], paired_bits, seq_index)
    owned = list(grad_terms)
    for member, buffer in zip(paired, narrowed):
        owned[member] = buffer
    top_term = grad_terms[level_count - 1]
    owned[level_count - 1] = lax.psum_scatter(top_term, "seq", scatter_dimension=0, tiled=True)
    key_acc = jnp.zeros((row_count, head_count, HD), jnp.float32)
    value_acc = jnp.zeros((row_count, head_count, HD), jnp.float32)
    for level_no in range(level_count):
        own_rows = owned[level_no]
        key_own = own_rows[:, : head_count * HD].reshape(-1, head_count, HD)
        value_own = own_rows[:, head_count * HD :].reshape(-1, head_count, HD)
        key_acc = key_acc + place_rows(key_own, level_masks[level_no])
        value_acc = value_acc + place_rows(value_own, level_masks[level_no])
    flat = (row_count, head_count * HD)
    return (
        attended.reshape(flat),
        query_acc.astype(jnp.bfloat16).reshape(flat),
        key_acc.astype(jnp.bfloat16).reshape(flat),
        value_acc.astype(jnp.bfloat16).reshape(flat),
    )


VMEM_BYTES = 56 * 2**20
NT = (((1,), (1,)), ((), ()))
TN = (((0,), (0,)), ((), ()))


def vmem_specs(count):
    return [pl.BlockSpec(memory_space=pltpu.VMEM)] * count


def head_columns(chip, offset):
    return pl.ds(pl.multiple_of((chip ^ offset) * HD, HD), HD)


def pack_kernel(chips, chip_ref, *refs):
    first, second = refs[:2]
    chip = chip_ref[0]
    for offset in range(chips):
        columns = head_columns(chip, offset)
        refs[2 + offset][0] = first[:, columns]
        refs[2 + offset][1] = second[:, columns]


def pack(chip, first, second, chips):
    rows = first.shape[0]
    block = jax.ShapeDtypeStruct((2, rows, HD), first.dtype)
    return pl.pallas_call(
        functools.partial(pack_kernel, chips),
        out_shape=[block] * chips,
        in_specs=[pl.BlockSpec(memory_space=pltpu.SMEM)] + vmem_specs(2),
        out_specs=vmem_specs(chips),
        compiler_params=pltpu.CompilerParams(vmem_limit_bytes=VMEM_BYTES),
        cost_estimate=pl.CostEstimate(flops=0, bytes_accessed=4 * first.size * 2, transcendentals=0),
        name="pack",
    )(chip, first, second)


def unpack_kernel(chips, chip_ref, *refs):
    chip = chip_ref[0]
    first, second = refs[chips : chips + 2]
    for offset in range(chips):
        columns = head_columns(chip, offset)
        first[:, columns] = refs[offset][0]
        second[:, columns] = refs[offset][1]


def unpack(chip, blocks):
    chips = len(blocks)
    rows = blocks[0].shape[1]
    whole = jax.ShapeDtypeStruct((rows, chips * HD), blocks[0].dtype)
    return pl.pallas_call(
        functools.partial(unpack_kernel, chips),
        out_shape=[whole] * 2,
        in_specs=[pl.BlockSpec(memory_space=pltpu.SMEM)] + vmem_specs(chips),
        out_specs=vmem_specs(2),
        compiler_params=pltpu.CompilerParams(vmem_limit_bytes=VMEM_BYTES),
        name="unpack",
    )(chip, *blocks)


def attention_kernel(chips, *refs):
    pairs = refs[: 2 * chips]
    query_grads = refs[2 * chips : 3 * chips]
    outs = refs[3 * chips : 4 * chips]
    own_ref, other_ref = refs[4 * chips : 4 * chips + 2]
    key_ref, value_ref, dkey_ref, dvalue_ref = refs[4 * chips + 2 :]
    rows = pairs[0].shape[1]
    for index, pair in enumerate(pairs):
        key_ref[index * rows : (index + 1) * rows] = pair[0]
        value_ref[index * rows : (index + 1) * rows] = pair[1]
    score_scale = HD ** (-0.5)
    exp_scale = score_scale * 1.4426950408889634
    key_all = key_ref[...]
    value_all = value_ref[...]
    for index in range(chips):
        query = query_grads[index][0]
        grad = query_grads[index][1]
        scores = lax.dot_general(query, key_all, NT, preferred_element_type=jnp.float32)
        row_peak = jnp.max(scores, axis=1, keepdims=True)
        probs = jnp.exp2(scores * exp_scale - row_peak * exp_scale)
        probs = probs * (1.0 / jnp.sum(probs, axis=1, keepdims=True))
        probs_low = probs.astype(jnp.bfloat16)
        attended = jnp.dot(probs_low, value_all, preferred_element_type=jnp.float32)
        attended = attended.astype(jnp.bfloat16)
        delta = jnp.sum(
            attended.astype(jnp.float32) * grad.astype(jnp.float32), axis=1, keepdims=True
        )
        dprobs = lax.dot_general(grad, value_all, NT, preferred_element_type=jnp.float32)
        dscore = (probs * (dprobs - delta)).astype(jnp.bfloat16)
        query_grad = jnp.dot(dscore, key_all, preferred_element_type=jnp.float32) * score_scale
        outs[index][0] = attended
        outs[index][1] = query_grad.astype(jnp.bfloat16)
        dkey = lax.dot_general(dscore, query, TN, preferred_element_type=jnp.float32)
        dvalue = lax.dot_general(probs_low, grad, TN, preferred_element_type=jnp.float32)
        if index == 0:
            dkey_ref[...] = dkey
            dvalue_ref[...] = dvalue
        else:
            dkey_ref[...] += dkey
            dvalue_ref[...] += dvalue
    half = chips * rows
    own_ref[0] = dkey_ref[:half] * score_scale
    own_ref[1] = dvalue_ref[:half]
    other_ref[0] = (dkey_ref[half:] * score_scale).astype(other_ref.dtype)
    other_ref[1] = dvalue_ref[half:].astype(other_ref.dtype)


def attention(pairs, query_grads):
    chips = len(query_grads)
    rows = pairs[0].shape[1]
    keys = 2 * chips * rows
    block = jax.ShapeDtypeStruct((2, rows, HD), jnp.bfloat16)
    products = chips * rows * keys * HD
    return pl.pallas_call(
        functools.partial(attention_kernel, chips),
        out_shape=[block] * chips
        + [
            jax.ShapeDtypeStruct((2, chips * rows, HD), jnp.float32),
            jax.ShapeDtypeStruct((2, chips * rows, HD), jnp.bfloat16),
        ],
        in_specs=vmem_specs(3 * chips),
        out_specs=vmem_specs(chips + 2),
        scratch_shapes=[
            pltpu.VMEM((keys, HD), jnp.bfloat16),
            pltpu.VMEM((keys, HD), jnp.bfloat16),
            pltpu.VMEM((keys, HD), jnp.float32),
            pltpu.VMEM((keys, HD), jnp.float32),
        ],
        compiler_params=pltpu.CompilerParams(vmem_limit_bytes=VMEM_BYTES),
        cost_estimate=pl.CostEstimate(
            flops=12 * products, bytes_accessed=6 * keys * HD * 2, transcendentals=chips * rows * keys
        ),
        name="attention",
    )(*pairs, *query_grads)


def add_kernel(chips, own_ref, other_ref, *outs):
    rows = outs[0].shape[1]
    for index in range(chips):
        part = slice(index * rows, (index + 1) * rows)
        outs[index][...] = (own_ref[:, part] + other_ref[:, part].astype(jnp.float32)).astype(
            jnp.bfloat16
        )


def add_partials(own, other, chips):
    rows = own.shape[1] // chips
    block = jax.ShapeDtypeStruct((2, rows, HD), jnp.bfloat16)
    return pl.pallas_call(
        functools.partial(add_kernel, chips),
        out_shape=[block] * chips,
        in_specs=vmem_specs(2),
        out_specs=vmem_specs(chips),
        compiler_params=pltpu.CompilerParams(vmem_limit_bytes=VMEM_BYTES),
        name="add_partials",
    )(own, other)


def to_chip(array, offset):
    return lax.ppermute(
        array, "seq", [(i, i ^ (2 * offset)) for i in range(lax.axis_size("seq"))]
    )


def to_core(array):
    return lax.ppermute(array, "seq", [(i, i ^ 1) for i in range(lax.axis_size("seq"))])


def exchange_order(chips):
    return [offset for offset in sorted(range(1, chips), key=lambda o: (-o.bit_length(), o))]


def exchange(blocks):
    moved = list(blocks)
    for offset in exchange_order(len(blocks)):
        moved[offset] = to_chip(blocks[offset], offset)
    return moved


def shards_one_level(query_rows, key_rows, value_rows, grad_output):
    chips = lax.axis_size("seq") // 2
    chip = (lax.axis_index("seq") // 2).reshape(1)
    pair_blocks = exchange(pack(chip, key_rows, value_rows, chips))
    query_blocks = exchange(pack(chip, query_rows, grad_output, chips))
    pair_blocks = pair_blocks + [to_core(block) for block in pair_blocks]
    *out_blocks, own, other = attention(pair_blocks, query_blocks)
    grad_blocks = add_partials(own, to_core(other), chips)
    attended, query_grad = unpack(chip, exchange(out_blocks))
    key_grad, value_grad = unpack(chip, exchange(grad_blocks))
    return (attended, query_grad, key_grad, value_grad)


def shards(query_rows, key_rows, value_rows, grad_output, dilation_offsets):
    seq_width = lax.axis_size("seq")
    if (
        dilation_offsets.shape[0] == 1
        and query_rows.shape[0] * seq_width == SEG
        and query_rows.shape[1] // HD * 2 == seq_width
    ):
        return shards_one_level(query_rows, key_rows, value_rows, grad_output)
    return shards_levels(query_rows, key_rows, value_rows, grad_output, dilation_offsets)


def solution(mesh):
    in_specs = (
        P(("groups", "seq"), "head"),
        P(("groups", "seq"), "head"),
        P(("groups", "seq"), "head"),
        P(("groups", "seq"), "head"),
        P(None, "head"),
    )
    out_specs = (
        P(("groups", "seq"), "head"),
        P(("groups", "seq"), "head"),
        P(("groups", "seq"), "head"),
        P(("groups", "seq"), "head"),
    )
    return jax.shard_map(shards, mesh=mesh, in_specs=in_specs, out_specs=out_specs, check_vma=False)
```

```python
import functools

import jax
import jax.numpy as jnp
from jax import lax
from jax.experimental import pallas as pl
from jax.experimental.pallas import tpu as pltpu
from jax.sharding import PartitionSpec as P

HD = 128
SEG = 2048


def shortened(array):

    def short(part):
        return part.astype(jnp.bfloat16) if part.dtype == jnp.float32 else part

    return jax.tree.map(short, array)


def from_partner(array, axis, stride):
    return lax.ppermute(array, axis, [(i, i ^ 1 << stride) for i in range(lax.axis_size(axis))])


def pick_rows(values, row_mask):
    stride = row_mask.shape[0]
    shaped = values.reshape((values.shape[0] // stride, stride) + values.shape[1:])
    mask_wide = row_mask.reshape(row_mask.shape + (1,) * (values.ndim - 2))
    return jnp.sum(jnp.where(mask_wide, shaped, jnp.zeros((), values.dtype)), axis=1)


def place_rows(values, row_mask):
    stride = row_mask.shape[0]
    mask_wide = row_mask.reshape(row_mask.shape + (1,) * (values.ndim - 2))
    spread = jnp.where(mask_wide, values[:, None], jnp.zeros((), values.dtype))
    return spread.reshape((values.shape[0] * stride,) + values.shape[1:])


def upper_of(seq_index, bit_number):
    return seq_index // 2**bit_number % 2 == 1


def widen_apart(buffers, bit_totals, seq_index):
    widened = []
    for buffer, bit_total in zip(buffers, bit_totals):
        for bit_number in range(bit_total):
            partner = jax.tree.map(
                lambda part, own: part.astype(own.dtype),
                from_partner(shortened(buffer), "seq", bit_number),
                buffer,
            )
            upper_side = upper_of(seq_index, bit_number)
            buffer = jnp.where(
                upper_side,
                jnp.concatenate([partner, buffer], 0),
                jnp.concatenate([buffer, partner], 0),
            )
        widened.append(buffer)
    return widened


def narrow_apart(buffers, bit_totals, seq_index):
    narrowed = []
    for buffer, bit_total in zip(buffers, bit_totals):
        for bit_number in reversed(range(bit_total)):
            half_rows = buffer.shape[0] // 2
            lower_half = buffer[:half_rows]
            upper_half = buffer[half_rows:]
            upper_side = upper_of(seq_index, bit_number)
            outgoing = jnp.where(upper_side, lower_half, upper_half)
            kept_half = jnp.where(upper_side, upper_half, lower_half)
            buffer = kept_half + from_partner(outgoing, "seq", bit_number)
        narrowed.append(buffer)
    return narrowed


def split_keys(gathered, head_count):
    width = head_count * HD
    key_all = gathered[:, :width].reshape(-1, head_count, HD)
    value_all = gathered[:, width : 2 * width].reshape(-1, head_count, HD)
    return (key_all, value_all)


def forward_level(query_part, gathered, head_count):
    score_scale = HD ** (-0.5)
    key_all, value_all = split_keys(gathered, head_count)
    scores = (
        jnp.einsum("nhd,khd->hnk", query_part, key_all, preferred_element_type=jnp.float32)
        * score_scale
    )
    row_peak = jnp.max(scores, axis=2, keepdims=True)
    row_sums = jnp.sum(jnp.exp(scores - row_peak), axis=2, keepdims=True)
    level_lse = row_peak + jnp.log(row_sums)
    level_probs = jnp.exp(scores - level_lse).astype(jnp.bfloat16)
    partial_value = jnp.einsum(
        "hnk,khd->nhd", level_probs, value_all, preferred_element_type=jnp.float32
    )
    return (partial_value, jnp.transpose(level_lse[:, :, 0]))


def backward_level(query_part, grad_part, total_part, delta_part, gathered, head_count):
    score_scale = HD ** (-0.5)
    key_all, value_all = split_keys(gathered, head_count)
    scores = (
        jnp.einsum("nhd,khd->hnk", query_part, key_all, preferred_element_type=jnp.float32)
        * score_scale
    )
    glob = jnp.exp(scores - jnp.transpose(total_part)[:, :, None])
    glob_low = glob.astype(jnp.bfloat16)
    value_part = jnp.einsum("hnk,nhd->khd", glob_low, grad_part, preferred_element_type=jnp.float32)
    dprob = jnp.einsum("nhd,khd->hnk", grad_part, value_all, preferred_element_type=jnp.float32)
    dscore = (glob * (dprob - jnp.transpose(delta_part)[:, :, None])).astype(jnp.bfloat16)
    query_part_grad = (
        jnp.einsum("hnk,khd->nhd", dscore, key_all, preferred_element_type=jnp.float32)
        * score_scale
    )
    key_part = (
        jnp.einsum("hnk,nhd->khd", dscore, query_part, preferred_element_type=jnp.float32)
        * score_scale
    )
    key_count = key_part.shape[0]
    grad_term = jnp.concatenate(
        [key_part.reshape(key_count, -1), value_part.reshape(key_count, -1)], axis=1
    )
    return (query_part_grad, grad_term)


def shards_levels(query_rows, key_rows, value_rows, grad_output, dilation_offsets):
    row_count = query_rows.shape[0]
    head_count = query_rows.shape[1] // HD
    level_count = dilation_offsets.shape[0]
    seq_index = lax.axis_index("seq")
    seq_width = lax.axis_size("seq")
    query_three = query_rows.reshape(row_count, head_count, HD)
    key_three = key_rows.reshape(row_count, head_count, HD)
    value_three = value_rows.reshape(row_count, head_count, HD)
    grad_three = grad_output.reshape(row_count, head_count, HD)
    level_masks = []
    full_masks = []
    query_parts = []
    kept_pieces = []
    segment_bits = []
    for level_no in range(level_count):
        stride = 2**level_no
        row_mask = (
            lax.broadcasted_iota(jnp.int32, (stride, head_count), 0)
            == dilation_offsets[level_no][None, :]
        )
        full_mask = (
            lax.broadcasted_iota(jnp.int32, (row_count, head_count), 0) % stride
            == dilation_offsets[level_no][None, :]
        )
        level_masks.append(row_mask)
        full_masks.append(full_mask)
        query_parts.append(pick_rows(query_three, row_mask))
        key_three_part = pick_rows(key_three, row_mask)
        value_three_part = pick_rows(value_three, row_mask)
        piece = jnp.concatenate(
            [
                key_three_part.reshape(row_count // stride, -1),
                value_three_part.reshape(row_count // stride, -1),
            ],
            axis=1,
        )
        kept_pieces.append(piece)
        segment_bits.append(
            min((SEG * stride // row_count).bit_length() - 1, seq_width.bit_length() - 1)
        )
    paired = list(range(level_count - 1))
    paired_bits = [segment_bits[member] for member in paired]
    widened = widen_apart([kept_pieces[member] for member in paired], paired_bits, seq_index)
    gathered = list(kept_pieces)
    for member, buffer in zip(paired, widened):
        gathered[member] = buffer
    gathered[level_count - 1] = lax.all_gather(
        kept_pieces[level_count - 1], "seq", axis=0, tiled=True
    )
    out_parts = []
    lse_full = []
    for level_no in range(level_count):
        partial_value, level_lse = forward_level(
            query_parts[level_no], gathered[level_no], head_count
        )
        out_parts.append(place_rows(partial_value, level_masks[level_no]))
        lse_full.append(place_rows(level_lse, level_masks[level_no]))
    row_peak = lse_full[0]
    for level_no in range(1, level_count):
        row_peak = jnp.maximum(
            row_peak, jnp.where(full_masks[level_no], lse_full[level_no], lse_full[0])
        )
    exp_total = jnp.zeros((row_count, head_count), jnp.float32)
    for level_no in range(level_count):
        exp_total = exp_total + jnp.where(
            full_masks[level_no], jnp.exp(lse_full[level_no] - row_peak), jnp.float32(0.0)
        )
    total_lse = row_peak + jnp.log(exp_total)
    combined = jnp.zeros((row_count, head_count, HD), jnp.float32)
    for level_no in range(level_count):
        weight = jnp.exp(lse_full[level_no] - total_lse)
        combined = combined + jnp.where(
            full_masks[level_no][:, :, None],
            weight[:, :, None] * out_parts[level_no],
            jnp.float32(0.0),
        )
    attended = combined.astype(jnp.bfloat16)
    delta = jnp.sum(attended.astype(jnp.float32) * grad_three.astype(jnp.float32), axis=2)
    query_acc = jnp.zeros((row_count, head_count, HD), jnp.float32)
    grad_terms = []
    for level_no in range(level_count):
        row_mask = level_masks[level_no]
        grad_part = pick_rows(grad_three, row_mask)
        total_part = pick_rows(total_lse, row_mask)
        delta_part = pick_rows(delta, row_mask)
        query_part_grad, grad_term = backward_level(
            query_parts[level_no], grad_part, total_part, delta_part, gathered[level_no], head_count
        )
        query_acc = query_acc + place_rows(query_part_grad, row_mask)
        grad_terms.append(grad_term)
    narrowed = narrow_apart([grad_terms[member] for member in paired], paired_bits, seq_index)
    owned = list(grad_terms)
    for member, buffer in zip(paired, narrowed):
        owned[member] = buffer
    top_term = grad_terms[level_count - 1]
    owned[level_count - 1] = lax.psum_scatter(top_term, "seq", scatter_dimension=0, tiled=True)
    key_acc = jnp.zeros((row_count, head_count, HD), jnp.float32)
    value_acc = jnp.zeros((row_count, head_count, HD), jnp.float32)
    for level_no in range(level_count):
        own_rows = owned[level_no]
        key_own = own_rows[:, : head_count * HD].reshape(-1, head_count, HD)
        value_own = own_rows[:, head_count * HD :].reshape(-1, head_count, HD)
        key_acc = key_acc + place_rows(key_own, level_masks[level_no])
        value_acc = value_acc + place_rows(value_own, level_masks[level_no])
    flat = (row_count, head_count * HD)
    return (
        attended.reshape(flat),
        query_acc.astype(jnp.bfloat16).reshape(flat),
        key_acc.astype(jnp.bfloat16).reshape(flat),
        value_acc.astype(jnp.bfloat16).reshape(flat),
    )


NT = (((1,), (1,)), ((), ()))
TN = (((0,), (0,)), ((), ()))
MIB = 2**20
FORWARD_ROWS = 128
BACKWARD_ROWS = 256


def vmem_specs(count):
    return [pl.BlockSpec(memory_space=pltpu.VMEM)] * count


def any_specs(count):
    return [pl.BlockSpec(memory_space=pl.ANY)] * count


def head_columns(chip, offset):
    return pl.ds(pl.multiple_of((chip ^ offset) * HD, HD), HD)


def pack(chip, arrays, offset):
    start = (chip[0] ^ offset) * HD
    return jnp.stack([lax.dynamic_slice_in_dim(array, start, HD, axis=1) for array in arrays])


def unpack_kernel(layout, chip_ref, *refs):
    count = max(max(arrays) for _, arrays in layout) + 1
    blocks, outs, sems = refs[: len(layout)], refs[len(layout) : -1], refs[-1]
    chip = chip_ref[0]
    copies = []
    for at, (offset, arrays) in enumerate(layout):
        for place, index in enumerate(arrays):
            copies.append(
                pltpu.make_async_copy(
                    blocks[at].at[place],
                    outs[index].at[:, head_columns(chip, offset)],
                    sems.at[at, place],
                )
            )
    for copy in copies:
        copy.start()
    for copy in copies:
        copy.wait()


def unpack(chip, blocks, layout, width):
    count = max(max(arrays) for _, arrays in layout) + 1
    rows = blocks[0].shape[1]
    return pl.pallas_call(
        functools.partial(unpack_kernel, layout),
        out_shape=[jax.ShapeDtypeStruct((rows, width), blocks[0].dtype)] * count,
        in_specs=[pl.BlockSpec(memory_space=pltpu.SMEM)] + any_specs(len(blocks)),
        out_specs=any_specs(count),
        scratch_shapes=[pltpu.SemaphoreType.DMA((len(layout), count))],
        compiler_params=pltpu.CompilerParams(vmem_limit_bytes=MIB),
        name="unpack",
    )(chip, *blocks)


def forward_kernel(chips, *refs):
    blocks = refs[: 2 * chips]
    outs = refs[2 * chips : 3 * chips]
    probs_ref, scale_ref, key_ref, value_ref = refs[3 * chips :]
    rows = blocks[0].shape[1]
    for index, block in enumerate(blocks):
        key_ref[index * rows : (index + 1) * rows] = block[0]
        value_ref[index * rows : (index + 1) * rows, :HD] = block[1]
    value_ref[:, HD:] = jnp.ones((value_ref.shape[0], HD), value_ref.dtype)
    exp_scale = HD ** (-0.5) * 1.4426950408889634
    key_all = key_ref[...]
    value_all = value_ref[...]
    step = min(FORWARD_ROWS, rows)
    for index in range(chips):
        for start in range(0, rows, step):
            query = blocks[index][2, start : start + step]
            scores = lax.dot_general(query, key_all, NT, preferred_element_type=jnp.float32)
            row_peak = jnp.max(scores, axis=1, keepdims=True)
            probs = jnp.exp2(scores * exp_scale - row_peak * exp_scale).astype(jnp.bfloat16)
            here = slice(index * rows + start, index * rows + start + step)
            probs_ref[here] = probs
            sums = jnp.dot(probs, value_all, preferred_element_type=jnp.float32)
            row_scale = 1.0 / sums[:, HD:]
            scale_ref[here] = row_scale
            outs[index][0, start : start + step] = (sums[:, :HD] * row_scale).astype(jnp.bfloat16)


def forward(blocks, chips):
    rows = blocks[0].shape[1]
    queries = chips * rows
    keys = 2 * queries
    products = queries * keys * HD
    return pl.pallas_call(
        functools.partial(forward_kernel, chips),
        out_shape=[jax.ShapeDtypeStruct((1, rows, HD), jnp.bfloat16)] * chips
        + [
            jax.ShapeDtypeStruct((queries, keys), jnp.bfloat16),
            jax.ShapeDtypeStruct((queries, HD), jnp.float32),
        ],
        in_specs=vmem_specs(2 * chips),
        out_specs=vmem_specs(chips + 2),
        scratch_shapes=[
            pltpu.VMEM((keys, HD), jnp.bfloat16),
            pltpu.VMEM((keys, 2 * HD), jnp.bfloat16),
        ],
        compiler_params=pltpu.CompilerParams(vmem_limit_bytes=20 * MIB),
        cost_estimate=pl.CostEstimate(
            flops=4 * products, bytes_accessed=8 * MIB, transcendentals=queries * keys
        ),
        name="forward",
    )(*blocks)


def backward_kernel(chips, first, *refs):
    blocks = refs[:chips]
    key_blocks = refs[chips : 2 * chips]
    attended = refs[2 * chips : 3 * chips]
    probs_ref, scale_ref = refs[3 * chips : 3 * chips + 2]
    if first:
        query_ref, pair_ref, key_ref, value_ref, dkey_ref, dvalue_ref = refs[3 * chips + 2 :]
    else:
        query_ref = refs[3 * chips + 2]
        outs = refs[3 * chips + 3 : 4 * chips + 3]
        pair_ref, key_ref, value_ref, dkey_ref, dvalue_ref = refs[4 * chips + 3 :]
    rows = blocks[0].shape[1]
    score_scale = HD ** (-0.5)
    for index, block in enumerate(key_blocks):
        key_ref[index * rows : (index + 1) * rows] = block[0]
        value_ref[index * rows : (index + 1) * rows] = block[1]
    key_all = key_ref[...]
    value_all = value_ref[...]
    columns = slice(chips * rows, 2 * chips * rows) if first else slice(0, chips * rows)
    step = min(BACKWARD_ROWS, rows)
    fresh = True
    for index in range(chips):
        for start in range(0, rows, step):
            part = slice(start, start + step)
            here = slice(index * rows + start, index * rows + start + step)
            query = blocks[index][2, part]
            grad = blocks[index][3, part].astype(jnp.float32) * scale_ref[here]
            grad = grad.astype(jnp.bfloat16)
            probs = probs_ref[here, columns]
            delta = jnp.sum(
                attended[index][0, part].astype(jnp.float32) * grad.astype(jnp.float32),
                axis=1,
                keepdims=True,
            )
            dprobs = lax.dot_general(grad, value_all, NT, preferred_element_type=jnp.float32)
            dscore = (probs.astype(jnp.float32) * (dprobs - delta)).astype(jnp.bfloat16)
            query_grad = jnp.dot(dscore, key_all, preferred_element_type=jnp.float32)
            if first:
                query_ref[here] = query_grad
            else:
                query_grad = (query_grad + query_ref[here]) * score_scale
                outs[index][0, part] = query_grad.astype(jnp.bfloat16)
            dkey = lax.dot_general(dscore, query, TN, preferred_element_type=jnp.float32)
            dvalue = lax.dot_general(probs, grad, TN, preferred_element_type=jnp.float32)
            if fresh:
                dkey_ref[...] = dkey
                dvalue_ref[...] = dvalue
                fresh = False
            else:
                dkey_ref[...] += dkey
                dvalue_ref[...] += dvalue
    pair_ref[0] = (dkey_ref[...] * score_scale).astype(pair_ref.dtype)
    pair_ref[1] = dvalue_ref[...].astype(pair_ref.dtype)


def backward(first, blocks, key_blocks, attended, probs, scale, query_terms=()):
    chips = len(blocks)
    rows = blocks[0].shape[1]
    queries = probs.shape[0]
    query_outs = [jax.ShapeDtypeStruct((queries, HD), jnp.float32)]
    if not first:
        query_outs = [jax.ShapeDtypeStruct((1, rows, HD), jnp.bfloat16)] * chips
    return pl.pallas_call(
        functools.partial(backward_kernel, chips, first),
        out_shape=query_outs
        + [jax.ShapeDtypeStruct((2, queries, HD), jnp.bfloat16 if first else jnp.float32)],
        in_specs=vmem_specs(3 * chips + 2 + len(query_terms)),
        out_specs=vmem_specs(len(query_outs) + 1),
        scratch_shapes=[
            pltpu.VMEM((queries, HD), jnp.bfloat16),
            pltpu.VMEM((queries, HD), jnp.bfloat16),
            pltpu.VMEM((queries, HD), jnp.float32),
            pltpu.VMEM((queries, HD), jnp.float32),
        ],
        compiler_params=pltpu.CompilerParams(vmem_limit_bytes=20 * MIB),
        cost_estimate=pl.CostEstimate(
            flops=8 * queries * queries * HD, bytes_accessed=4 * MIB, transcendentals=0
        ),
        name="backward",
    )(*blocks, *key_blocks, *attended, probs, scale, *query_terms)


def add_kernel(chips, own_ref, other_ref, *refs):
    outs = refs[-chips:]
    rows = outs[0].shape[1]
    for index, out in enumerate(outs):
        part = slice(index * rows, (index + 1) * rows)
        total = own_ref[:, part] + other_ref[:, part].astype(jnp.float32)
        out[0:2] = total.astype(jnp.bfloat16)
        out[2] = refs[index][0]
        if out.shape[0] == 4:
            out[3] = refs[chips + index][0]


def add_partials(own, other, query_blocks, attended_near):
    chips = len(query_blocks)
    rows = own.shape[1] // chips
    return pl.pallas_call(
        functools.partial(add_kernel, chips),
        out_shape=[
            jax.ShapeDtypeStruct((4 if index < len(attended_near) else 3, rows, HD), jnp.bfloat16)
            for index in range(chips)
        ],
        in_specs=vmem_specs(2 + chips + len(attended_near)),
        out_specs=vmem_specs(chips),
        compiler_params=pltpu.CompilerParams(vmem_limit_bytes=8 * MIB),
        cost_estimate=pl.CostEstimate(
            flops=own.size, bytes_accessed=8 * own.size, transcendentals=0
        ),
        name="add_partials",
    )(own, other, *query_blocks, *attended_near)


def to_chip(array, offset):
    return lax.ppermute(
        array, "seq", [(i, i ^ (2 * offset)) for i in range(lax.axis_size("seq"))]
    )


def to_core(array):
    return lax.ppermute(array, "seq", [(i, i ^ 1) for i in range(lax.axis_size("seq"))])


def shards_one_level(query_rows, key_rows, value_rows, grad_output):
    chips = lax.axis_size("seq") // 2
    chip = (lax.axis_index("seq") // 2).reshape(1)
    far = sorted(range(2, chips), key=lambda offset: (-offset.bit_length(), offset))
    arrays = [key_rows, value_rows, query_rows, grad_output]
    blocks = [None] * chips
    for offset in far + [1]:
        blocks[offset] = to_chip(pack(chip, arrays, offset), offset)
    blocks[0] = pack(chip, arrays, 0)
    others = [to_core(block) for block in blocks]
    *attended, probs, scale = forward(blocks + others, chips)
    query_terms, other = backward(True, blocks, others, attended, probs, scale)
    other = to_core(other)
    *query_blocks, own = backward(False, blocks, blocks, attended, probs, scale, [query_terms])
    outs = add_partials(own, other, query_blocks, attended)
    moved = [outs[0]] + [to_chip(outs[offset], offset) for offset in range(1, chips)]
    out_blocks = moved
    out_layout = [(offset, (2, 3, 1, 0)[: outs[offset].shape[0]]) for offset in range(chips)]
    return tuple(unpack(chip, out_blocks, out_layout, query_rows.shape[1]))


def shards(query_rows, key_rows, value_rows, grad_output, dilation_offsets):
    seq_width = lax.axis_size("seq")
    if (
        dilation_offsets.shape[0] == 1
        and query_rows.shape[0] * seq_width == SEG
        and query_rows.shape[1] // HD * 2 == seq_width
    ):
        return shards_one_level(query_rows, key_rows, value_rows, grad_output)
    return shards_levels(query_rows, key_rows, value_rows, grad_output, dilation_offsets)


def solution(mesh):
    in_specs = (
        P(("groups", "seq"), "head"),
        P(("groups", "seq"), "head"),
        P(("groups", "seq"), "head"),
        P(("groups", "seq"), "head"),
        P(None, "head"),
    )
    out_specs = (
        P(("groups", "seq"), "head"),
        P(("groups", "seq"), "head"),
        P(("groups", "seq"), "head"),
        P(("groups", "seq"), "head"),
    )
    return jax.shard_map(shards, mesh=mesh, in_specs=in_specs, out_specs=out_specs, check_vma=False)
```

```python
import functools

import jax
import jax.numpy as jnp
from jax import lax
from jax.experimental import pallas as pl
from jax.experimental.pallas import tpu as pltpu
from jax.sharding import PartitionSpec as P

HD = 128
SEG = 2048


def shortened(array):

    def short(part):
        return part.astype(jnp.bfloat16) if part.dtype == jnp.float32 else part

    return jax.tree.map(short, array)


def from_partner(array, axis, stride):
    return lax.ppermute(array, axis, [(i, i ^ 1 << stride) for i in range(lax.axis_size(axis))])


def pick_rows(values, row_mask):
    stride = row_mask.shape[0]
    shaped = values.reshape((values.shape[0] // stride, stride) + values.shape[1:])
    mask_wide = row_mask.reshape(row_mask.shape + (1,) * (values.ndim - 2))
    return jnp.sum(jnp.where(mask_wide, shaped, jnp.zeros((), values.dtype)), axis=1)


def place_rows(values, row_mask):
    stride = row_mask.shape[0]
    mask_wide = row_mask.reshape(row_mask.shape + (1,) * (values.ndim - 2))
    spread = jnp.where(mask_wide, values[:, None], jnp.zeros((), values.dtype))
    return spread.reshape((values.shape[0] * stride,) + values.shape[1:])


def upper_of(seq_index, bit_number):
    return seq_index // 2**bit_number % 2 == 1


def widen_apart(buffers, bit_totals, seq_index):
    widened = []
    for buffer, bit_total in zip(buffers, bit_totals):
        for bit_number in range(bit_total):
            partner = jax.tree.map(
                lambda part, own: part.astype(own.dtype),
                from_partner(shortened(buffer), "seq", bit_number),
                buffer,
            )
            upper_side = upper_of(seq_index, bit_number)
            buffer = jnp.where(
                upper_side,
                jnp.concatenate([partner, buffer], 0),
                jnp.concatenate([buffer, partner], 0),
            )
        widened.append(buffer)
    return widened


def narrow_apart(buffers, bit_totals, seq_index):
    narrowed = []
    for buffer, bit_total in zip(buffers, bit_totals):
        for bit_number in reversed(range(bit_total)):
            half_rows = buffer.shape[0] // 2
            lower_half = buffer[:half_rows]
            upper_half = buffer[half_rows:]
            upper_side = upper_of(seq_index, bit_number)
            outgoing = jnp.where(upper_side, lower_half, upper_half)
            kept_half = jnp.where(upper_side, upper_half, lower_half)
            buffer = kept_half + from_partner(outgoing, "seq", bit_number)
        narrowed.append(buffer)
    return narrowed


def split_keys(gathered, head_count):
    width = head_count * HD
    key_all = gathered[:, :width].reshape(-1, head_count, HD)
    value_all = gathered[:, width : 2 * width].reshape(-1, head_count, HD)
    return (key_all, value_all)


def forward_level(query_part, gathered, head_count):
    score_scale = HD ** (-0.5)
    key_all, value_all = split_keys(gathered, head_count)
    scores = (
        jnp.einsum("nhd,khd->hnk", query_part, key_all, preferred_element_type=jnp.float32)
        * score_scale
    )
    row_peak = jnp.max(scores, axis=2, keepdims=True)
    row_sums = jnp.sum(jnp.exp(scores - row_peak), axis=2, keepdims=True)
    level_lse = row_peak + jnp.log(row_sums)
    level_probs = jnp.exp(scores - level_lse).astype(jnp.bfloat16)
    partial_value = jnp.einsum(
        "hnk,khd->nhd", level_probs, value_all, preferred_element_type=jnp.float32
    )
    return (partial_value, jnp.transpose(level_lse[:, :, 0]))


def backward_level(query_part, grad_part, total_part, delta_part, gathered, head_count):
    score_scale = HD ** (-0.5)
    key_all, value_all = split_keys(gathered, head_count)
    scores = (
        jnp.einsum("nhd,khd->hnk", query_part, key_all, preferred_element_type=jnp.float32)
        * score_scale
    )
    glob = jnp.exp(scores - jnp.transpose(total_part)[:, :, None])
    glob_low = glob.astype(jnp.bfloat16)
    value_part = jnp.einsum("hnk,nhd->khd", glob_low, grad_part, preferred_element_type=jnp.float32)
    dprob = jnp.einsum("nhd,khd->hnk", grad_part, value_all, preferred_element_type=jnp.float32)
    dscore = (glob * (dprob - jnp.transpose(delta_part)[:, :, None])).astype(jnp.bfloat16)
    query_part_grad = (
        jnp.einsum("hnk,khd->nhd", dscore, key_all, preferred_element_type=jnp.float32)
        * score_scale
    )
    key_part = (
        jnp.einsum("hnk,nhd->khd", dscore, query_part, preferred_element_type=jnp.float32)
        * score_scale
    )
    key_count = key_part.shape[0]
    grad_term = jnp.concatenate(
        [key_part.reshape(key_count, -1), value_part.reshape(key_count, -1)], axis=1
    )
    return (query_part_grad, grad_term)


def shards_levels(query_rows, key_rows, value_rows, grad_output, dilation_offsets):
    row_count = query_rows.shape[0]
    head_count = query_rows.shape[1] // HD
    level_count = dilation_offsets.shape[0]
    seq_index = lax.axis_index("seq")
    seq_width = lax.axis_size("seq")
    query_three = query_rows.reshape(row_count, head_count, HD)
    key_three = key_rows.reshape(row_count, head_count, HD)
    value_three = value_rows.reshape(row_count, head_count, HD)
    grad_three = grad_output.reshape(row_count, head_count, HD)
    level_masks = []
    full_masks = []
    query_parts = []
    kept_pieces = []
    segment_bits = []
    for level_no in range(level_count):
        stride = 2**level_no
        row_mask = (
            lax.broadcasted_iota(jnp.int32, (stride, head_count), 0)
            == dilation_offsets[level_no][None, :]
        )
        full_mask = (
            lax.broadcasted_iota(jnp.int32, (row_count, head_count), 0) % stride
            == dilation_offsets[level_no][None, :]
        )
        level_masks.append(row_mask)
        full_masks.append(full_mask)
        query_parts.append(pick_rows(query_three, row_mask))
        key_three_part = pick_rows(key_three, row_mask)
        value_three_part = pick_rows(value_three, row_mask)
        piece = jnp.concatenate(
            [
                key_three_part.reshape(row_count // stride, -1),
                value_three_part.reshape(row_count // stride, -1),
            ],
            axis=1,
        )
        kept_pieces.append(piece)
        segment_bits.append(
            min((SEG * stride // row_count).bit_length() - 1, seq_width.bit_length() - 1)
        )
    paired = list(range(level_count - 1))
    paired_bits = [segment_bits[member] for member in paired]
    widened = widen_apart([kept_pieces[member] for member in paired], paired_bits, seq_index)
    gathered = list(kept_pieces)
    for member, buffer in zip(paired, widened):
        gathered[member] = buffer
    gathered[level_count - 1] = lax.all_gather(
        kept_pieces[level_count - 1], "seq", axis=0, tiled=True
    )
    out_parts = []
    lse_full = []
    for level_no in range(level_count):
        partial_value, level_lse = forward_level(
            query_parts[level_no], gathered[level_no], head_count
        )
        out_parts.append(place_rows(partial_value, level_masks[level_no]))
        lse_full.append(place_rows(level_lse, level_masks[level_no]))
    row_peak = lse_full[0]
    for level_no in range(1, level_count):
        row_peak = jnp.maximum(
            row_peak, jnp.where(full_masks[level_no], lse_full[level_no], lse_full[0])
        )
    exp_total = jnp.zeros((row_count, head_count), jnp.float32)
    for level_no in range(level_count):
        exp_total = exp_total + jnp.where(
            full_masks[level_no], jnp.exp(lse_full[level_no] - row_peak), jnp.float32(0.0)
        )
    total_lse = row_peak + jnp.log(exp_total)
    combined = jnp.zeros((row_count, head_count, HD), jnp.float32)
    for level_no in range(level_count):
        weight = jnp.exp(lse_full[level_no] - total_lse)
        combined = combined + jnp.where(
            full_masks[level_no][:, :, None],
            weight[:, :, None] * out_parts[level_no],
            jnp.float32(0.0),
        )
    attended = combined.astype(jnp.bfloat16)
    delta = jnp.sum(attended.astype(jnp.float32) * grad_three.astype(jnp.float32), axis=2)
    query_acc = jnp.zeros((row_count, head_count, HD), jnp.float32)
    grad_terms = []
    for level_no in range(level_count):
        row_mask = level_masks[level_no]
        grad_part = pick_rows(grad_three, row_mask)
        total_part = pick_rows(total_lse, row_mask)
        delta_part = pick_rows(delta, row_mask)
        query_part_grad, grad_term = backward_level(
            query_parts[level_no], grad_part, total_part, delta_part, gathered[level_no], head_count
        )
        query_acc = query_acc + place_rows(query_part_grad, row_mask)
        grad_terms.append(grad_term)
    narrowed = narrow_apart([grad_terms[member] for member in paired], paired_bits, seq_index)
    owned = list(grad_terms)
    for member, buffer in zip(paired, narrowed):
        owned[member] = buffer
    top_term = grad_terms[level_count - 1]
    owned[level_count - 1] = lax.psum_scatter(top_term, "seq", scatter_dimension=0, tiled=True)
    key_acc = jnp.zeros((row_count, head_count, HD), jnp.float32)
    value_acc = jnp.zeros((row_count, head_count, HD), jnp.float32)
    for level_no in range(level_count):
        own_rows = owned[level_no]
        key_own = own_rows[:, : head_count * HD].reshape(-1, head_count, HD)
        value_own = own_rows[:, head_count * HD :].reshape(-1, head_count, HD)
        key_acc = key_acc + place_rows(key_own, level_masks[level_no])
        value_acc = value_acc + place_rows(value_own, level_masks[level_no])
    flat = (row_count, head_count * HD)
    return (
        attended.reshape(flat),
        query_acc.astype(jnp.bfloat16).reshape(flat),
        key_acc.astype(jnp.bfloat16).reshape(flat),
        value_acc.astype(jnp.bfloat16).reshape(flat),
    )


NT = (((1,), (1,)), ((), ()))
TN = (((0,), (0,)), ((), ()))
MIB = 2**20
FORWARD_ROWS = 128
BACKWARD_ROWS = 256
SCORE_SCALE = HD ** (-0.5)
EXP_SCALE = SCORE_SCALE * 1.4426950408889634


def vmem_specs(count):
    return [pl.BlockSpec(memory_space=pltpu.VMEM)] * count


def any_specs(count):
    return [pl.BlockSpec(memory_space=pl.ANY)] * count


def head_columns(chip, offset):
    return pl.ds(pl.multiple_of((chip ^ offset) * HD, HD), HD)


def pack(chip, arrays, offset):
    start = (chip[0] ^ offset) * HD
    return jnp.stack([lax.dynamic_slice_in_dim(array, start, HD, axis=1) for array in arrays])


def unpack_kernel(layout, chip_ref, *refs):
    count = max(max(arrays) for _, arrays in layout) + 1
    blocks, outs, sems = refs[: len(layout)], refs[len(layout) : -1], refs[-1]
    chip = chip_ref[0]
    copies = []
    for at, (offset, arrays) in enumerate(layout):
        for place, index in enumerate(arrays):
            copies.append(
                pltpu.make_async_copy(
                    blocks[at].at[place],
                    outs[index].at[:, head_columns(chip, offset)],
                    sems.at[at, place],
                )
            )
    for copy in copies:
        copy.start()
    for copy in copies:
        copy.wait()


def unpack(chip, blocks, layout, width):
    count = max(max(arrays) for _, arrays in layout) + 1
    rows = blocks[0].shape[1]
    return pl.pallas_call(
        functools.partial(unpack_kernel, layout),
        out_shape=[jax.ShapeDtypeStruct((rows, width), blocks[0].dtype)] * count,
        in_specs=[pl.BlockSpec(memory_space=pltpu.SMEM)] + any_specs(len(blocks)),
        out_specs=any_specs(count),
        scratch_shapes=[pltpu.SemaphoreType.DMA((len(layout), count))],
        compiler_params=pltpu.CompilerParams(vmem_limit_bytes=MIB),
        name="unpack",
    )(chip, *blocks)


def load_keys(blocks, key_ref, value_ref):
    rows = blocks[0].shape[1]
    for index, block in enumerate(blocks):
        key_ref[index * rows : (index + 1) * rows] = block[0]
        value_ref[index * rows : (index + 1) * rows, :HD] = block[1]
    if value_ref.shape[1] > HD:
        value_ref[:, HD:] = jnp.ones((value_ref.shape[0], HD), value_ref.dtype)


def forward_rows(query, key_all, value_ones):
    scores = lax.dot_general(query, key_all, NT, preferred_element_type=jnp.float32)
    row_peak = jnp.max(scores, axis=1, keepdims=True)
    probs = jnp.exp2(scores * EXP_SCALE - row_peak * EXP_SCALE).astype(jnp.bfloat16)
    sums = jnp.dot(probs, value_ones, preferred_element_type=jnp.float32)
    row_scale = 1.0 / sums[:, HD:]
    return probs, row_scale, (sums[:, :HD] * row_scale).astype(jnp.bfloat16)


def query_pair(block, part):
    first = block.shape[0] - 2
    return block[first, part], block[first + 1, part]


def scaled_grad(grad, row_scale, attended):
    grad = (grad.astype(jnp.float32) * row_scale).astype(jnp.bfloat16)
    products = attended.astype(jnp.float32) * grad.astype(jnp.float32)
    return grad, jnp.sum(products, axis=1, keepdims=True)


def backward_rows(query, grad, delta, probs, key_part, value_part):
    dprobs = lax.dot_general(grad, value_part, NT, preferred_element_type=jnp.float32)
    dscore = (probs.astype(jnp.float32) * (dprobs - delta)).astype(jnp.bfloat16)
    return (
        jnp.dot(dscore, key_part, preferred_element_type=jnp.float32),
        lax.dot_general(dscore, query, TN, preferred_element_type=jnp.float32),
        lax.dot_general(probs, grad, TN, preferred_element_type=jnp.float32),
    )


def forward_pass(query_blocks, outs, key_ref, value_ref, probs_ref, scale_ref):
    rows = outs[0].shape[1]
    step = min(FORWARD_ROWS, rows)
    key_all = key_ref[...]
    value_ones = value_ref[...]
    for index, block in enumerate(query_blocks):
        for start in range(0, rows, step):
            part = slice(start, start + step)
            here = slice(index * rows + start, index * rows + start + step)
            probs, row_scale, attended = forward_rows(
                query_pair(block, part)[0], key_all, value_ones
            )
            probs_ref[here] = probs
            scale_ref[here] = row_scale
            outs[index][0, part] = attended


def row_parts(query_blocks, rows):
    step = min(BACKWARD_ROWS, rows)
    for index in range(len(query_blocks)):
        for start in range(0, rows, step):
            first = index * rows + start
            yield index, slice(start, start + step), slice(first, first + step)


def near_kernel(chips, near, *refs):
    pair_blocks, refs = refs[: 2 * chips], refs[2 * chips :]
    outs, query_outs, refs = refs[:near], refs[near : 2 * near], refs[2 * near :]
    terms_ref, key_ref, value_ref, probs_ref, scale_ref = refs
    query_blocks = pair_blocks[:near]
    rows = outs[0].shape[1]
    load_keys(pair_blocks, key_ref, value_ref)
    forward_pass(query_blocks, outs, key_ref, value_ref, probs_ref, scale_ref)
    for index, part, here in row_parts(query_blocks, rows):
        query, grad = query_pair(query_blocks[index], part)
        grad, delta = scaled_grad(
            grad, scale_ref[here], outs[index][0, part]
        )
        dquery, dkey, dvalue = backward_rows(
            query, grad, delta, probs_ref[here], key_ref[...], value_ref[:, :HD]
        )
        query_outs[index][0, part] = (dquery * SCORE_SCALE).astype(jnp.bfloat16)
        if here.start == 0:
            terms_ref[0] = dkey
            terms_ref[1] = dvalue
        else:
            terms_ref[0] += dkey
            terms_ref[1] += dvalue


def far_kernel(chips, far, *refs):
    pair_blocks, query_blocks, refs = refs[: 2 * chips], refs[2 * chips :][:far], refs[2 * chips + far :]
    near_ref, outs, refs = refs[0], refs[1 : 1 + far], refs[1 + far :]
    probs_out, scale_ref, query_terms, other_ref = refs[:4]
    key_ref, value_ref, probs_ref, terms_ref = refs[4:]
    rows = outs[0].shape[1]
    half = chips * rows
    load_keys(pair_blocks, key_ref, value_ref)
    forward_pass(query_blocks, outs, key_ref, value_ref, probs_ref, scale_ref)
    terms_ref[...] = near_ref[:, half:]
    for index, part, here in row_parts(query_blocks, rows):
        query, grad = query_pair(query_blocks[index], part)
        grad, delta = scaled_grad(
            grad, scale_ref[here], outs[index][0, part]
        )
        probs_out[here] = probs_ref[here, :half]
        dquery, dkey, dvalue = backward_rows(
            query, grad, delta, probs_ref[here, half:], key_ref[half:], value_ref[half:, :HD]
        )
        query_terms[here] = dquery
        terms_ref[0] += dkey
        terms_ref[1] += dvalue
    other_ref[0] = (terms_ref[0] * SCORE_SCALE).astype(other_ref.dtype)
    other_ref[1] = terms_ref[1].astype(other_ref.dtype)


def own_kernel(chips, far, *refs):
    pair_blocks, query_blocks, refs = refs[:chips], refs[chips:][:far], refs[chips + far :]
    attended, refs = refs[:far], refs[far:]
    near_ref, probs_ref, scale_ref, query_terms = refs[:4]
    query_outs, refs = refs[4 : 4 + far], refs[4 + far :]
    own_ref, key_ref, value_ref = refs
    rows = attended[0].shape[1]
    half = chips * rows
    load_keys(pair_blocks, key_ref, value_ref)
    own_ref[...] = near_ref[:, :half]
    for index, part, here in row_parts(query_blocks, rows):
        query, grad = query_pair(query_blocks[index], part)
        grad, delta = scaled_grad(
            grad, scale_ref[here], attended[index][0, part]
        )
        dquery, dkey, dvalue = backward_rows(
            query, grad, delta, probs_ref[here], key_ref[...], value_ref[...]
        )
        dquery = (dquery + query_terms[here]) * SCORE_SCALE
        query_outs[index][0, part] = dquery.astype(jnp.bfloat16)
        own_ref[0] += dkey
        own_ref[1] += dvalue
    own_ref[0] *= SCORE_SCALE


def call_vmem(kernel, name, operands, outs, scratch, products, limit):
    return pl.pallas_call(
        kernel,
        out_shape=[jax.ShapeDtypeStruct(shape, dtype) for shape, dtype in outs],
        in_specs=vmem_specs(len(operands)),
        out_specs=vmem_specs(len(outs)),
        scratch_shapes=[pltpu.VMEM(shape, dtype) for shape, dtype in scratch],
        compiler_params=pltpu.CompilerParams(vmem_limit_bytes=limit),
        cost_estimate=pl.CostEstimate(flops=2 * products, bytes_accessed=MIB, transcendentals=0),
        name=name,
    )(*operands)


def add_kernel(chips, own_ref, other_ref, *refs):
    query_blocks, attended, outs = refs[:chips], refs[chips : 2 * chips], refs[2 * chips :]
    rows = outs[0].shape[1]
    for index, out in enumerate(outs):
        part = slice(index * rows, (index + 1) * rows)
        total = own_ref[:, part] + other_ref[:, part].astype(jnp.float32)
        out[0] = attended[index][0]
        out[1] = query_blocks[index][0]
        out[2:4] = total.astype(jnp.bfloat16)


def to_chip(array, offset):
    return lax.ppermute(
        array, "seq", [(i, i ^ (2 * offset)) for i in range(lax.axis_size("seq"))]
    )


def to_core(array):
    return lax.ppermute(array, "seq", [(i, i ^ 1) for i in range(lax.axis_size("seq"))])


def after(array, other):
    return lax.optimization_barrier((array, other))[0]


def shards_one_level(query_rows, key_rows, value_rows, grad_output):
    bf16, f32 = jnp.bfloat16, jnp.float32
    chips = lax.axis_size("seq") // 2
    near = 2
    far = chips - near
    rows = query_rows.shape[0]
    half, keys = chips * rows, 2 * chips * rows
    chip = (lax.axis_index("seq") // 2).reshape(1)
    pairs = [key_rows, value_rows]
    queries = [query_rows, grad_output]
    wanted = [(offset, pairs) for offset in range(near, chips)]
    wanted += [(1, pairs + queries), (0, pairs + queries)]
    wanted += [(offset, queries) for offset in range(near, chips)]
    packed = []
    for offset, arrays in wanted:
        packed.append(pack(chip, arrays, offset))
        chip = after(chip, packed[-1])
    moved = [to_chip(block, offset) if offset else block for block, (offset, _) in zip(packed, wanted)]
    pair_blocks = [moved[far + 1], moved[far]] + moved[:far]
    query_blocks = moved[far + 2 :]
    all_blocks = pair_blocks + [to_core(block) for block in pair_blocks]
    block = ((1, rows, HD), bf16)
    product = near * rows * keys * HD
    *outs, terms = call_vmem(
        functools.partial(near_kernel, chips, near),
        "near",
        all_blocks,
        [block] * (2 * near) + [((2, keys, HD), f32)],
        [((keys, HD), bf16), ((keys, 2 * HD), bf16), ((near * rows, keys), bf16), ((near * rows, HD), f32)],
        6 * product,
        24 * MIB,
    )
    attended, query_grads = outs[:near], outs[near:]
    product = far * rows * half * HD
    *outs, probs, scale, query_terms, other = call_vmem(
        functools.partial(far_kernel, chips, far),
        "far",
        all_blocks + query_blocks + [terms],
        [block] * far
        + [((far * rows, half), bf16), ((far * rows, HD), f32), ((far * rows, HD), f32), ((2, half, HD), bf16)],
        [((keys, HD), bf16), ((keys, 2 * HD), bf16), ((far * rows, keys), bf16), ((2, half, HD), f32)],
        8 * product,
        24 * MIB,
    )
    other = to_core(other)
    attended = attended + outs
    *outs, own = call_vmem(
        functools.partial(own_kernel, chips, far),
        "own",
        pair_blocks + query_blocks + outs + [terms, probs, scale, query_terms],
        [block] * far + [((2, half, HD), f32)],
        [((half, HD), bf16), ((half, HD), bf16)],
        4 * product,
        16 * MIB,
    )
    query_grads = query_grads + outs
    outs = call_vmem(
        functools.partial(add_kernel, chips),
        "add_partials",
        [own, other] + query_grads + attended,
        [((4, rows, HD), bf16)] * chips,
        [],
        rows,
        8 * MIB,
    )
    order = list(range(near, chips)) + [1]
    returned = [outs[0]] + [to_chip(outs[offset], offset) for offset in order]
    layout = [(offset, (0, 1, 2, 3)) for offset in [0] + order]
    return tuple(unpack(chip, returned, layout, query_rows.shape[1]))


def shards(query_rows, key_rows, value_rows, grad_output, dilation_offsets):
    seq_width = lax.axis_size("seq")
    if (
        dilation_offsets.shape[0] == 1
        and query_rows.shape[0] * seq_width == SEG
        and query_rows.shape[1] // HD * 2 == seq_width
    ):
        return shards_one_level(query_rows, key_rows, value_rows, grad_output)
    return shards_levels(query_rows, key_rows, value_rows, grad_output, dilation_offsets)


def solution(mesh):
    in_specs = (
        P(("groups", "seq"), "head"),
        P(("groups", "seq"), "head"),
        P(("groups", "seq"), "head"),
        P(("groups", "seq"), "head"),
        P(None, "head"),
    )
    out_specs = (
        P(("groups", "seq"), "head"),
        P(("groups", "seq"), "head"),
        P(("groups", "seq"), "head"),
        P(("groups", "seq"), "head"),
    )
    return jax.shard_map(shards, mesh=mesh, in_specs=in_specs, out_specs=out_specs, check_vma=False)
```

```python
import functools

import jax
import jax.numpy as jnp
from jax import lax
from jax.experimental import pallas as pl
from jax.experimental.pallas import tpu as pltpu
from jax.sharding import PartitionSpec as P

HD = 128
SEG = 2048


def shortened(array):

    def short(part):
        return part.astype(jnp.bfloat16) if part.dtype == jnp.float32 else part

    return jax.tree.map(short, array)


def from_partner(array, axis, stride):
    return lax.ppermute(array, axis, [(i, i ^ 1 << stride) for i in range(lax.axis_size(axis))])


def pick_rows(values, row_mask):
    stride = row_mask.shape[0]
    shaped = values.reshape((values.shape[0] // stride, stride) + values.shape[1:])
    mask_wide = row_mask.reshape(row_mask.shape + (1,) * (values.ndim - 2))
    return jnp.sum(jnp.where(mask_wide, shaped, jnp.zeros((), values.dtype)), axis=1)


def place_rows(values, row_mask):
    stride = row_mask.shape[0]
    mask_wide = row_mask.reshape(row_mask.shape + (1,) * (values.ndim - 2))
    spread = jnp.where(mask_wide, values[:, None], jnp.zeros((), values.dtype))
    return spread.reshape((values.shape[0] * stride,) + values.shape[1:])


def upper_of(seq_index, bit_number):
    return seq_index // 2**bit_number % 2 == 1


def widen_apart(buffers, bit_totals, seq_index):
    widened = []
    for buffer, bit_total in zip(buffers, bit_totals):
        for bit_number in range(bit_total):
            partner = jax.tree.map(
                lambda part, own: part.astype(own.dtype),
                from_partner(shortened(buffer), "seq", bit_number),
                buffer,
            )
            upper_side = upper_of(seq_index, bit_number)
            buffer = jnp.where(
                upper_side,
                jnp.concatenate([partner, buffer], 0),
                jnp.concatenate([buffer, partner], 0),
            )
        widened.append(buffer)
    return widened


def narrow_apart(buffers, bit_totals, seq_index):
    narrowed = []
    for buffer, bit_total in zip(buffers, bit_totals):
        for bit_number in reversed(range(bit_total)):
            half_rows = buffer.shape[0] // 2
            lower_half = buffer[:half_rows]
            upper_half = buffer[half_rows:]
            upper_side = upper_of(seq_index, bit_number)
            outgoing = jnp.where(upper_side, lower_half, upper_half)
            kept_half = jnp.where(upper_side, upper_half, lower_half)
            buffer = kept_half + from_partner(outgoing, "seq", bit_number)
        narrowed.append(buffer)
    return narrowed


def split_keys(gathered, head_count):
    width = head_count * HD
    key_all = gathered[:, :width].reshape(-1, head_count, HD)
    value_all = gathered[:, width : 2 * width].reshape(-1, head_count, HD)
    return (key_all, value_all)


def forward_level(query_part, gathered, head_count):
    score_scale = HD ** (-0.5)
    key_all, value_all = split_keys(gathered, head_count)
    scores = (
        jnp.einsum("nhd,khd->hnk", query_part, key_all, preferred_element_type=jnp.float32)
        * score_scale
    )
    row_peak = jnp.max(scores, axis=2, keepdims=True)
    row_sums = jnp.sum(jnp.exp(scores - row_peak), axis=2, keepdims=True)
    level_lse = row_peak + jnp.log(row_sums)
    level_probs = jnp.exp(scores - level_lse).astype(jnp.bfloat16)
    partial_value = jnp.einsum(
        "hnk,khd->nhd", level_probs, value_all, preferred_element_type=jnp.float32
    )
    return (partial_value, jnp.transpose(level_lse[:, :, 0]))


def backward_level(query_part, grad_part, total_part, delta_part, gathered, head_count):
    score_scale = HD ** (-0.5)
    key_all, value_all = split_keys(gathered, head_count)
    scores = (
        jnp.einsum("nhd,khd->hnk", query_part, key_all, preferred_element_type=jnp.float32)
        * score_scale
    )
    glob = jnp.exp(scores - jnp.transpose(total_part)[:, :, None])
    glob_low = glob.astype(jnp.bfloat16)
    value_part = jnp.einsum("hnk,nhd->khd", glob_low, grad_part, preferred_element_type=jnp.float32)
    dprob = jnp.einsum("nhd,khd->hnk", grad_part, value_all, preferred_element_type=jnp.float32)
    dscore = (glob * (dprob - jnp.transpose(delta_part)[:, :, None])).astype(jnp.bfloat16)
    query_part_grad = (
        jnp.einsum("hnk,khd->nhd", dscore, key_all, preferred_element_type=jnp.float32)
        * score_scale
    )
    key_part = (
        jnp.einsum("hnk,nhd->khd", dscore, query_part, preferred_element_type=jnp.float32)
        * score_scale
    )
    key_count = key_part.shape[0]
    grad_term = jnp.concatenate(
        [key_part.reshape(key_count, -1), value_part.reshape(key_count, -1)], axis=1
    )
    return (query_part_grad, grad_term)


def shards_levels(query_rows, key_rows, value_rows, grad_output, dilation_offsets):
    row_count = query_rows.shape[0]
    head_count = query_rows.shape[1] // HD
    level_count = dilation_offsets.shape[0]
    seq_index = lax.axis_index("seq")
    seq_width = lax.axis_size("seq")
    query_three = query_rows.reshape(row_count, head_count, HD)
    key_three = key_rows.reshape(row_count, head_count, HD)
    value_three = value_rows.reshape(row_count, head_count, HD)
    grad_three = grad_output.reshape(row_count, head_count, HD)
    level_masks = []
    full_masks = []
    query_parts = []
    kept_pieces = []
    segment_bits = []
    for level_no in range(level_count):
        stride = 2**level_no
        row_mask = (
            lax.broadcasted_iota(jnp.int32, (stride, head_count), 0)
            == dilation_offsets[level_no][None, :]
        )
        full_mask = (
            lax.broadcasted_iota(jnp.int32, (row_count, head_count), 0) % stride
            == dilation_offsets[level_no][None, :]
        )
        level_masks.append(row_mask)
        full_masks.append(full_mask)
        query_parts.append(pick_rows(query_three, row_mask))
        key_three_part = pick_rows(key_three, row_mask)
        value_three_part = pick_rows(value_three, row_mask)
        piece = jnp.concatenate(
            [
                key_three_part.reshape(row_count // stride, -1),
                value_three_part.reshape(row_count // stride, -1),
            ],
            axis=1,
        )
        kept_pieces.append(piece)
        segment_bits.append(
            min((SEG * stride // row_count).bit_length() - 1, seq_width.bit_length() - 1)
        )
    paired = list(range(level_count - 1))
    paired_bits = [segment_bits[member] for member in paired]
    widened = widen_apart([kept_pieces[member] for member in paired], paired_bits, seq_index)
    gathered = list(kept_pieces)
    for member, buffer in zip(paired, widened):
        gathered[member] = buffer
    gathered[level_count - 1] = lax.all_gather(
        kept_pieces[level_count - 1], "seq", axis=0, tiled=True
    )
    out_parts = []
    lse_full = []
    for level_no in range(level_count):
        partial_value, level_lse = forward_level(
            query_parts[level_no], gathered[level_no], head_count
        )
        out_parts.append(place_rows(partial_value, level_masks[level_no]))
        lse_full.append(place_rows(level_lse, level_masks[level_no]))
    row_peak = lse_full[0]
    for level_no in range(1, level_count):
        row_peak = jnp.maximum(
            row_peak, jnp.where(full_masks[level_no], lse_full[level_no], lse_full[0])
        )
    exp_total = jnp.zeros((row_count, head_count), jnp.float32)
    for level_no in range(level_count):
        exp_total = exp_total + jnp.where(
            full_masks[level_no], jnp.exp(lse_full[level_no] - row_peak), jnp.float32(0.0)
        )
    total_lse = row_peak + jnp.log(exp_total)
    combined = jnp.zeros((row_count, head_count, HD), jnp.float32)
    for level_no in range(level_count):
        weight = jnp.exp(lse_full[level_no] - total_lse)
        combined = combined + jnp.where(
            full_masks[level_no][:, :, None],
            weight[:, :, None] * out_parts[level_no],
            jnp.float32(0.0),
        )
    attended = combined.astype(jnp.bfloat16)
    delta = jnp.sum(attended.astype(jnp.float32) * grad_three.astype(jnp.float32), axis=2)
    query_acc = jnp.zeros((row_count, head_count, HD), jnp.float32)
    grad_terms = []
    for level_no in range(level_count):
        row_mask = level_masks[level_no]
        grad_part = pick_rows(grad_three, row_mask)
        total_part = pick_rows(total_lse, row_mask)
        delta_part = pick_rows(delta, row_mask)
        query_part_grad, grad_term = backward_level(
            query_parts[level_no], grad_part, total_part, delta_part, gathered[level_no], head_count
        )
        query_acc = query_acc + place_rows(query_part_grad, row_mask)
        grad_terms.append(grad_term)
    narrowed = narrow_apart([grad_terms[member] for member in paired], paired_bits, seq_index)
    owned = list(grad_terms)
    for member, buffer in zip(paired, narrowed):
        owned[member] = buffer
    top_term = grad_terms[level_count - 1]
    owned[level_count - 1] = lax.psum_scatter(top_term, "seq", scatter_dimension=0, tiled=True)
    key_acc = jnp.zeros((row_count, head_count, HD), jnp.float32)
    value_acc = jnp.zeros((row_count, head_count, HD), jnp.float32)
    for level_no in range(level_count):
        own_rows = owned[level_no]
        key_own = own_rows[:, : head_count * HD].reshape(-1, head_count, HD)
        value_own = own_rows[:, head_count * HD :].reshape(-1, head_count, HD)
        key_acc = key_acc + place_rows(key_own, level_masks[level_no])
        value_acc = value_acc + place_rows(value_own, level_masks[level_no])
    flat = (row_count, head_count * HD)
    return (
        attended.reshape(flat),
        query_acc.astype(jnp.bfloat16).reshape(flat),
        key_acc.astype(jnp.bfloat16).reshape(flat),
        value_acc.astype(jnp.bfloat16).reshape(flat),
    )


NT = (((1,), (1,)), ((), ()))
TN = (((0,), (0,)), ((), ()))
MIB = 2**20
FORWARD_ROWS = 128
BACKWARD_ROWS = 256
SCORE_SCALE = HD ** (-0.5)
EXP_SCALE = SCORE_SCALE * 1.4426950408889634


def vmem_specs(count):
    return [pl.BlockSpec(memory_space=pltpu.VMEM)] * count


def any_specs(count):
    return [pl.BlockSpec(memory_space=pl.ANY)] * count


def head_columns(chip, offset):
    return pl.ds(pl.multiple_of((chip ^ offset) * HD, HD), HD)


def pack(chip, arrays, offset):
    start = (chip[0] ^ offset) * HD
    return jnp.stack([lax.dynamic_slice_in_dim(array, start, HD, axis=1) for array in arrays])


def unpack_kernel(layout, chip_ref, *refs):
    count = max(max(arrays) for _, arrays in layout) + 1
    blocks, outs, sems = refs[: len(layout)], refs[len(layout) : -1], refs[-1]
    chip = chip_ref[0]
    copies = []
    for at, (offset, arrays) in enumerate(layout):
        for place, index in enumerate(arrays):
            copies.append(
                pltpu.make_async_copy(
                    blocks[at].at[place],
                    outs[index].at[:, head_columns(chip, offset)],
                    sems.at[at, place],
                )
            )
    for copy in copies:
        copy.start()
    for copy in copies:
        copy.wait()


def unpack(chip, blocks, layout, width):
    count = max(max(arrays) for _, arrays in layout) + 1
    rows = blocks[0].shape[1]
    return pl.pallas_call(
        functools.partial(unpack_kernel, layout),
        out_shape=[jax.ShapeDtypeStruct((rows, width), blocks[0].dtype)] * count,
        in_specs=[pl.BlockSpec(memory_space=pltpu.SMEM)] + any_specs(len(blocks)),
        out_specs=any_specs(count),
        scratch_shapes=[pltpu.SemaphoreType.DMA((len(layout), count))],
        compiler_params=pltpu.CompilerParams(vmem_limit_bytes=MIB),
        name="unpack",
    )(chip, *blocks)


def load_keys(blocks, key_ref, value_ref):
    rows = blocks[0].shape[1]
    for index, block in enumerate(blocks):
        key_ref[index * rows : (index + 1) * rows] = block[0]
        value_ref[index * rows : (index + 1) * rows, :HD] = block[1]
    if value_ref.shape[1] > HD:
        value_ref[:, HD:] = jnp.ones((value_ref.shape[0], HD), value_ref.dtype)


def forward_rows(query, key_all, value_ones):
    scores = lax.dot_general(query, key_all, NT, preferred_element_type=jnp.float32)
    row_peak = jnp.max(scores, axis=1, keepdims=True)
    probs = jnp.exp2(scores * EXP_SCALE - row_peak * EXP_SCALE).astype(jnp.bfloat16)
    sums = jnp.dot(probs, value_ones, preferred_element_type=jnp.float32)
    row_scale = 1.0 / sums[:, HD:]
    return probs, row_scale, (sums[:, :HD] * row_scale).astype(jnp.bfloat16)


def query_pair(block, part):
    first = block.shape[0] - 2
    return block[first, part], block[first + 1, part]


def scaled_grad(grad, row_scale, attended):
    grad = (grad.astype(jnp.float32) * row_scale).astype(jnp.bfloat16)
    products = attended.astype(jnp.float32) * grad.astype(jnp.float32)
    return grad, jnp.sum(products, axis=1, keepdims=True)


def backward_rows(query, grad, delta, probs, key_part, value_part):
    dprobs = lax.dot_general(grad, value_part, NT, preferred_element_type=jnp.float32)
    dscore = (probs.astype(jnp.float32) * (dprobs - delta)).astype(jnp.bfloat16)
    return (
        jnp.dot(dscore, key_part, preferred_element_type=jnp.float32),
        lax.dot_general(dscore, query, TN, preferred_element_type=jnp.float32),
        lax.dot_general(probs, grad, TN, preferred_element_type=jnp.float32),
    )


def forward_pass(query_blocks, outs, key_ref, value_ref, probs_ref, scale_ref):
    rows = outs[0].shape[1]
    step = min(FORWARD_ROWS, rows)
    key_all = key_ref[...]
    value_ones = value_ref[...]
    for index, block in enumerate(query_blocks):
        for start in range(0, rows, step):
            part = slice(start, start + step)
            here = slice(index * rows + start, index * rows + start + step)
            probs, row_scale, attended = forward_rows(
                query_pair(block, part)[0], key_all, value_ones
            )
            probs_ref[here] = probs
            scale_ref[here] = row_scale
            outs[index][0, part] = attended


def row_parts(query_blocks, rows):
    step = min(BACKWARD_ROWS, rows)
    for index in range(len(query_blocks)):
        for start in range(0, rows, step):
            first = index * rows + start
            yield index, slice(start, start + step), slice(first, first + step)


def add_terms(terms_ref, given_ref, dkey, dvalue):
    terms_ref[0] = dkey if given_ref is None else given_ref[0] + dkey
    terms_ref[1] = dvalue if given_ref is None else given_ref[1] + dvalue


def near_kernel(chips, near, *refs):
    pair_blocks, refs = refs[: 2 * chips], refs[2 * chips :]
    outs, query_outs, refs = refs[:near], refs[near : 2 * near], refs[2 * near :]
    own_ref, other_ref, key_ref, value_ref, probs_ref, scale_ref = refs
    query_blocks = pair_blocks[:near]
    rows = outs[0].shape[1]
    half = chips * rows
    load_keys(pair_blocks, key_ref, value_ref)
    forward_pass(query_blocks, outs, key_ref, value_ref, probs_ref, scale_ref)
    for index, part, here in row_parts(query_blocks, rows):
        query, grad = query_pair(query_blocks[index], part)
        grad, delta = scaled_grad(grad, scale_ref[here], outs[index][0, part])
        dquery, dkey, dvalue = backward_rows(
            query, grad, delta, probs_ref[here], key_ref[...], value_ref[:, :HD]
        )
        query_outs[index][0, part] = (dquery * SCORE_SCALE).astype(jnp.bfloat16)
        add_terms(own_ref, own_ref if here.start else None, dkey[:half], dvalue[:half])
        add_terms(other_ref, other_ref if here.start else None, dkey[half:], dvalue[half:])


def far_kernel(half, key_ref, value_ref, block_ref, given_ref, out, probs_out, scale_ref, query_terms, other_ref, probs_ref, terms_ref):
    forward_pass([block_ref], [out], key_ref, value_ref, probs_ref, scale_ref)
    probs_out[...] = probs_ref[:, :half]
    for index, part, here in row_parts([block_ref], out.shape[1]):
        query, grad = query_pair(block_ref, part)
        grad, delta = scaled_grad(grad, scale_ref[here], out[0, part])
        dquery, dkey, dvalue = backward_rows(
            query, grad, delta, probs_ref[here, half:], key_ref[half:], value_ref[half:, :HD]
        )
        query_terms[here] = dquery
        add_terms(terms_ref, terms_ref if here.start else given_ref, dkey, dvalue)
    last = other_ref.dtype == jnp.bfloat16
    other_ref[0] = (terms_ref[0] * (SCORE_SCALE if last else 1.0)).astype(other_ref.dtype)
    other_ref[1] = terms_ref[1].astype(other_ref.dtype)


def own_kernel(half, far, *refs):
    key_ref, value_ref, given_ref, refs = *refs[:3], refs[3:]
    query_blocks, attended, probs, scale, query_terms = (
        refs[at * far : (at + 1) * far] for at in range(5)
    )
    query_outs, own_ref = refs[5 * far : -1], refs[-1]
    for index, block_ref in enumerate(query_blocks):
        for _, part, here in row_parts([block_ref], attended[index].shape[1]):
            query, grad = query_pair(block_ref, part)
            grad, delta = scaled_grad(grad, scale[index][here], attended[index][0, part])
            dquery, dkey, dvalue = backward_rows(
                query, grad, delta, probs[index][here], key_ref[:half], value_ref[:half, :HD]
            )
            dquery = (dquery + query_terms[index][here]) * SCORE_SCALE
            query_outs[index][0, part] = dquery.astype(jnp.bfloat16)
            fresh = index == 0 and here.start == 0
            add_terms(own_ref, given_ref if fresh else own_ref, dkey, dvalue)
    own_ref[0] *= SCORE_SCALE


def call_vmem(kernel, name, operands, outs, scratch, products, limit):
    return pl.pallas_call(
        kernel,
        out_shape=[jax.ShapeDtypeStruct(shape, dtype) for shape, dtype in outs],
        in_specs=vmem_specs(len(operands)),
        out_specs=vmem_specs(len(outs)),
        scratch_shapes=[pltpu.VMEM(shape, dtype) for shape, dtype in scratch],
        compiler_params=pltpu.CompilerParams(vmem_limit_bytes=limit),
        cost_estimate=pl.CostEstimate(flops=2 * products, bytes_accessed=MIB, transcendentals=0),
        name=name,
    )(*operands)


def add_kernel(chips, own_ref, other_ref, *refs):
    query_blocks, attended, outs = refs[:chips], refs[chips : 2 * chips], refs[2 * chips :]
    rows = outs[0].shape[1]
    for index, out in enumerate(outs):
        part = slice(index * rows, (index + 1) * rows)
        total = own_ref[:, part] + other_ref[:, part].astype(jnp.float32)
        out[0] = attended[index][0]
        out[1] = query_blocks[index][0]
        out[2:4] = total.astype(jnp.bfloat16)


def to_chip(array, offset):
    return lax.ppermute(
        array, "seq", [(i, i ^ (2 * offset)) for i in range(lax.axis_size("seq"))]
    )


def to_core(array):
    return lax.ppermute(array, "seq", [(i, i ^ 1) for i in range(lax.axis_size("seq"))])


def after(array, other):
    return lax.optimization_barrier((array, other))[0]


def shards_one_level(query_rows, key_rows, value_rows, grad_output):
    bf16, f32 = jnp.bfloat16, jnp.float32
    chips = lax.axis_size("seq") // 2
    near = 2
    far = chips - near
    rows = query_rows.shape[0]
    half, keys = chips * rows, 2 * chips * rows
    chip = (lax.axis_index("seq") // 2).reshape(1)
    pairs = [key_rows, value_rows]
    queries = [query_rows, grad_output]
    wanted = [("keys", offset, pairs) for offset in range(2, chips)]
    wanted += [("keys", offset, pairs + queries) for offset in (1, 0)]
    wanted += [("queries", offset, queries) for offset in range(2, chips)]
    moved = {}
    for name, offset, arrays in wanted:
        packed = pack(chip, arrays, offset)
        chip = after(chip, packed)
        moved[name, offset] = to_chip(packed, offset) if offset else packed
    pair_blocks = [moved["keys", offset] for offset in range(chips)]
    query_blocks = [moved["queries", offset] for offset in range(near, chips)]
    all_blocks = pair_blocks + [to_core(value) for value in pair_blocks]
    block = ((1, rows, HD), bf16)
    terms = ((2, half, HD), f32)
    *outs, own, other, key_all, value_ones = call_vmem(
        functools.partial(near_kernel, chips, near),
        "near",
        all_blocks,
        [block] * (2 * near) + [terms, terms, ((keys, HD), bf16), ((keys, 2 * HD), bf16)],
        [((near * rows, keys), bf16), ((near * rows, HD), f32)],
        6 * near * rows * keys * HD,
        20 * MIB,
    )
    attended, query_grads = outs[:near], outs[near:]
    parts = []
    for index in range(far):
        last = index == far - 1
        *part, other = call_vmem(
            functools.partial(far_kernel, half),
            "far",
            [key_all, value_ones, query_blocks[index], other],
            [block, ((rows, half), bf16), ((rows, HD), f32), ((rows, HD), f32), ((2, half, HD), bf16 if last else f32)],
            [((rows, keys), bf16), ((2, half, HD), f32)],
            8 * rows * half * HD,
            16 * MIB,
        )
        parts.append(part)
    other = to_core(other)
    columns = [list(column) for column in zip(*parts)]
    attended = attended + columns[0]
    *outs, own = call_vmem(
        functools.partial(own_kernel, half, far),
        "own",
        [key_all, value_ones, own] + query_blocks + sum(columns, []),
        [block] * far + [terms],
        [],
        4 * far * rows * half * HD,
        16 * MIB,
    )
    query_grads = query_grads + outs
    outs = call_vmem(
        functools.partial(add_kernel, chips),
        "add_partials",
        [own, other] + query_grads + attended,
        [((4, rows, HD), bf16)] * chips,
        [],
        rows,
        8 * MIB,
    )
    order = list(range(chips - 1, 0, -1))
    returned = [outs[0]] + [to_chip(outs[offset], offset) for offset in order]
    layout = [(offset, (0, 1, 2, 3)) for offset in [0] + order]
    return tuple(unpack(chip, returned, layout, query_rows.shape[1]))


def shards(query_rows, key_rows, value_rows, grad_output, dilation_offsets):
    seq_width = lax.axis_size("seq")
    if (
        dilation_offsets.shape[0] == 1
        and query_rows.shape[0] * seq_width == SEG
        and query_rows.shape[1] // HD * 2 == seq_width
    ):
        return shards_one_level(query_rows, key_rows, value_rows, grad_output)
    return shards_levels(query_rows, key_rows, value_rows, grad_output, dilation_offsets)


def solution(mesh):
    in_specs = (
        P(("groups", "seq"), "head"),
        P(("groups", "seq"), "head"),
        P(("groups", "seq"), "head"),
        P(("groups", "seq"), "head"),
        P(None, "head"),
    )
    out_specs = (
        P(("groups", "seq"), "head"),
        P(("groups", "seq"), "head"),
        P(("groups", "seq"), "head"),
        P(("groups", "seq"), "head"),
    )
    return jax.shard_map(shards, mesh=mesh, in_specs=in_specs, out_specs=out_specs, check_vma=False)
```

```python
import functools

import jax
import jax.numpy as jnp
from jax import lax
from jax.experimental import pallas as pl
from jax.experimental.pallas import tpu as pltpu
from jax.sharding import PartitionSpec as P

HD = 128
SEG = 2048


def shortened(array):

    def short(part):
        return part.astype(jnp.bfloat16) if part.dtype == jnp.float32 else part

    return jax.tree.map(short, array)


def from_partner(array, axis, stride):
    return lax.ppermute(array, axis, [(i, i ^ 1 << stride) for i in range(lax.axis_size(axis))])


def pick_rows(values, row_mask):
    stride = row_mask.shape[0]
    shaped = values.reshape((values.shape[0] // stride, stride) + values.shape[1:])
    mask_wide = row_mask.reshape(row_mask.shape + (1,) * (values.ndim - 2))
    return jnp.sum(jnp.where(mask_wide, shaped, jnp.zeros((), values.dtype)), axis=1)


def place_rows(values, row_mask):
    stride = row_mask.shape[0]
    mask_wide = row_mask.reshape(row_mask.shape + (1,) * (values.ndim - 2))
    spread = jnp.where(mask_wide, values[:, None], jnp.zeros((), values.dtype))
    return spread.reshape((values.shape[0] * stride,) + values.shape[1:])


def upper_of(seq_index, bit_number):
    return seq_index // 2**bit_number % 2 == 1


def widen_apart(buffers, bit_totals, seq_index):
    widened = []
    for buffer, bit_total in zip(buffers, bit_totals):
        for bit_number in range(bit_total):
            partner = jax.tree.map(
                lambda part, own: part.astype(own.dtype),
                from_partner(shortened(buffer), "seq", bit_number),
                buffer,
            )
            upper_side = upper_of(seq_index, bit_number)
            buffer = jnp.where(
                upper_side,
                jnp.concatenate([partner, buffer], 0),
                jnp.concatenate([buffer, partner], 0),
            )
        widened.append(buffer)
    return widened


def narrow_apart(buffers, bit_totals, seq_index):
    narrowed = []
    for buffer, bit_total in zip(buffers, bit_totals):
        for bit_number in reversed(range(bit_total)):
            half_rows = buffer.shape[0] // 2
            lower_half = buffer[:half_rows]
            upper_half = buffer[half_rows:]
            upper_side = upper_of(seq_index, bit_number)
            outgoing = jnp.where(upper_side, lower_half, upper_half)
            kept_half = jnp.where(upper_side, upper_half, lower_half)
            buffer = kept_half + from_partner(outgoing, "seq", bit_number)
        narrowed.append(buffer)
    return narrowed


def split_keys(gathered, head_count):
    width = head_count * HD
    key_all = gathered[:, :width].reshape(-1, head_count, HD)
    value_all = gathered[:, width : 2 * width].reshape(-1, head_count, HD)
    return (key_all, value_all)


def forward_level(query_part, gathered, head_count):
    score_scale = HD ** (-0.5)
    key_all, value_all = split_keys(gathered, head_count)
    scores = (
        jnp.einsum("nhd,khd->hnk", query_part, key_all, preferred_element_type=jnp.float32)
        * score_scale
    )
    row_peak = jnp.max(scores, axis=2, keepdims=True)
    row_sums = jnp.sum(jnp.exp(scores - row_peak), axis=2, keepdims=True)
    level_lse = row_peak + jnp.log(row_sums)
    level_probs = jnp.exp(scores - level_lse).astype(jnp.bfloat16)
    partial_value = jnp.einsum(
        "hnk,khd->nhd", level_probs, value_all, preferred_element_type=jnp.float32
    )
    return (partial_value, jnp.transpose(level_lse[:, :, 0]))


def backward_level(query_part, grad_part, total_part, delta_part, gathered, head_count):
    score_scale = HD ** (-0.5)
    key_all, value_all = split_keys(gathered, head_count)
    scores = (
        jnp.einsum("nhd,khd->hnk", query_part, key_all, preferred_element_type=jnp.float32)
        * score_scale
    )
    glob = jnp.exp(scores - jnp.transpose(total_part)[:, :, None])
    glob_low = glob.astype(jnp.bfloat16)
    value_part = jnp.einsum("hnk,nhd->khd", glob_low, grad_part, preferred_element_type=jnp.float32)
    dprob = jnp.einsum("nhd,khd->hnk", grad_part, value_all, preferred_element_type=jnp.float32)
    dscore = (glob * (dprob - jnp.transpose(delta_part)[:, :, None])).astype(jnp.bfloat16)
    query_part_grad = (
        jnp.einsum("hnk,khd->nhd", dscore, key_all, preferred_element_type=jnp.float32)
        * score_scale
    )
    key_part = (
        jnp.einsum("hnk,nhd->khd", dscore, query_part, preferred_element_type=jnp.float32)
        * score_scale
    )
    key_count = key_part.shape[0]
    grad_term = jnp.concatenate(
        [key_part.reshape(key_count, -1), value_part.reshape(key_count, -1)], axis=1
    )
    return (query_part_grad, grad_term)


def shards_levels(query_rows, key_rows, value_rows, grad_output, dilation_offsets):
    row_count = query_rows.shape[0]
    head_count = query_rows.shape[1] // HD
    level_count = dilation_offsets.shape[0]
    seq_index = lax.axis_index("seq")
    seq_width = lax.axis_size("seq")
    query_three = query_rows.reshape(row_count, head_count, HD)
    key_three = key_rows.reshape(row_count, head_count, HD)
    value_three = value_rows.reshape(row_count, head_count, HD)
    grad_three = grad_output.reshape(row_count, head_count, HD)
    level_masks = []
    full_masks = []
    query_parts = []
    kept_pieces = []
    segment_bits = []
    for level_no in range(level_count):
        stride = 2**level_no
        row_mask = (
            lax.broadcasted_iota(jnp.int32, (stride, head_count), 0)
            == dilation_offsets[level_no][None, :]
        )
        full_mask = (
            lax.broadcasted_iota(jnp.int32, (row_count, head_count), 0) % stride
            == dilation_offsets[level_no][None, :]
        )
        level_masks.append(row_mask)
        full_masks.append(full_mask)
        query_parts.append(pick_rows(query_three, row_mask))
        key_three_part = pick_rows(key_three, row_mask)
        value_three_part = pick_rows(value_three, row_mask)
        piece = jnp.concatenate(
            [
                key_three_part.reshape(row_count // stride, -1),
                value_three_part.reshape(row_count // stride, -1),
            ],
            axis=1,
        )
        kept_pieces.append(piece)
        segment_bits.append(
            min((SEG * stride // row_count).bit_length() - 1, seq_width.bit_length() - 1)
        )
    paired = list(range(level_count - 1))
    paired_bits = [segment_bits[member] for member in paired]
    widened = widen_apart([kept_pieces[member] for member in paired], paired_bits, seq_index)
    gathered = list(kept_pieces)
    for member, buffer in zip(paired, widened):
        gathered[member] = buffer
    gathered[level_count - 1] = lax.all_gather(
        kept_pieces[level_count - 1], "seq", axis=0, tiled=True
    )
    out_parts = []
    lse_full = []
    for level_no in range(level_count):
        partial_value, level_lse = forward_level(
            query_parts[level_no], gathered[level_no], head_count
        )
        out_parts.append(place_rows(partial_value, level_masks[level_no]))
        lse_full.append(place_rows(level_lse, level_masks[level_no]))
    row_peak = lse_full[0]
    for level_no in range(1, level_count):
        row_peak = jnp.maximum(
            row_peak, jnp.where(full_masks[level_no], lse_full[level_no], lse_full[0])
        )
    exp_total = jnp.zeros((row_count, head_count), jnp.float32)
    for level_no in range(level_count):
        exp_total = exp_total + jnp.where(
            full_masks[level_no], jnp.exp(lse_full[level_no] - row_peak), jnp.float32(0.0)
        )
    total_lse = row_peak + jnp.log(exp_total)
    combined = jnp.zeros((row_count, head_count, HD), jnp.float32)
    for level_no in range(level_count):
        weight = jnp.exp(lse_full[level_no] - total_lse)
        combined = combined + jnp.where(
            full_masks[level_no][:, :, None],
            weight[:, :, None] * out_parts[level_no],
            jnp.float32(0.0),
        )
    attended = combined.astype(jnp.bfloat16)
    delta = jnp.sum(attended.astype(jnp.float32) * grad_three.astype(jnp.float32), axis=2)
    query_acc = jnp.zeros((row_count, head_count, HD), jnp.float32)
    grad_terms = []
    for level_no in range(level_count):
        row_mask = level_masks[level_no]
        grad_part = pick_rows(grad_three, row_mask)
        total_part = pick_rows(total_lse, row_mask)
        delta_part = pick_rows(delta, row_mask)
        query_part_grad, grad_term = backward_level(
            query_parts[level_no], grad_part, total_part, delta_part, gathered[level_no], head_count
        )
        query_acc = query_acc + place_rows(query_part_grad, row_mask)
        grad_terms.append(grad_term)
    narrowed = narrow_apart([grad_terms[member] for member in paired], paired_bits, seq_index)
    owned = list(grad_terms)
    for member, buffer in zip(paired, narrowed):
        owned[member] = buffer
    top_term = grad_terms[level_count - 1]
    owned[level_count - 1] = lax.psum_scatter(top_term, "seq", scatter_dimension=0, tiled=True)
    key_acc = jnp.zeros((row_count, head_count, HD), jnp.float32)
    value_acc = jnp.zeros((row_count, head_count, HD), jnp.float32)
    for level_no in range(level_count):
        own_rows = owned[level_no]
        key_own = own_rows[:, : head_count * HD].reshape(-1, head_count, HD)
        value_own = own_rows[:, head_count * HD :].reshape(-1, head_count, HD)
        key_acc = key_acc + place_rows(key_own, level_masks[level_no])
        value_acc = value_acc + place_rows(value_own, level_masks[level_no])
    flat = (row_count, head_count * HD)
    return (
        attended.reshape(flat),
        query_acc.astype(jnp.bfloat16).reshape(flat),
        key_acc.astype(jnp.bfloat16).reshape(flat),
        value_acc.astype(jnp.bfloat16).reshape(flat),
    )


NT = (((1,), (1,)), ((), ()))
TN = (((0,), (0,)), ((), ()))
MIB = 2**20
FORWARD_ROWS = 128
BACKWARD_ROWS = 256
SCORE_SCALE = HD ** (-0.5)
EXP_SCALE = SCORE_SCALE * 1.4426950408889634


def vmem_specs(count):
    return [pl.BlockSpec(memory_space=pltpu.VMEM)] * count


def any_specs(count):
    return [pl.BlockSpec(memory_space=pl.ANY)] * count


def head_columns(chip, offset):
    return pl.ds(pl.multiple_of((chip ^ offset) * HD, HD), HD)


def pack(chip, arrays, offset):
    start = (chip[0] ^ offset) * HD
    return jnp.stack([lax.dynamic_slice_in_dim(array, start, HD, axis=1) for array in arrays])


def unpack_kernel(layout, chip_ref, *refs):
    count = max(max(arrays) for _, arrays in layout) + 1
    blocks, outs, sems = refs[: len(layout)], refs[len(layout) : -1], refs[-1]
    chip = chip_ref[0]
    copies = []
    for at, (offset, arrays) in enumerate(layout):
        for place, index in enumerate(arrays):
            copies.append(
                pltpu.make_async_copy(
                    blocks[at].at[place],
                    outs[index].at[:, head_columns(chip, offset)],
                    sems.at[at, place],
                )
            )
    for copy in copies:
        copy.start()
    for copy in copies:
        copy.wait()


def unpack(chip, blocks, layout, width):
    count = max(max(arrays) for _, arrays in layout) + 1
    rows = blocks[0].shape[1]
    return pl.pallas_call(
        functools.partial(unpack_kernel, layout),
        out_shape=[jax.ShapeDtypeStruct((rows, width), blocks[0].dtype)] * count,
        in_specs=[pl.BlockSpec(memory_space=pltpu.SMEM)] + any_specs(len(blocks)),
        out_specs=any_specs(count),
        scratch_shapes=[pltpu.SemaphoreType.DMA((len(layout), count))],
        compiler_params=pltpu.CompilerParams(vmem_limit_bytes=MIB),
        name="unpack",
    )(chip, *blocks)


def load_keys(blocks, key_ref, value_ref):
    rows = blocks[0].shape[1]
    for index, block in enumerate(blocks):
        key_ref[index * rows : (index + 1) * rows] = block[0]
        value_ref[index * rows : (index + 1) * rows, :HD] = block[1]
    if value_ref.shape[1] > HD:
        value_ref[:, HD:] = jnp.ones((value_ref.shape[0], HD), value_ref.dtype)


def forward_rows(query, key_all, value_ones):
    scores = lax.dot_general(query, key_all, NT, preferred_element_type=jnp.float32)
    row_peak = jnp.max(scores, axis=1, keepdims=True)
    probs = jnp.exp2(scores * EXP_SCALE - row_peak * EXP_SCALE).astype(jnp.bfloat16)
    sums = jnp.dot(probs, value_ones, preferred_element_type=jnp.float32)
    row_scale = 1.0 / sums[:, HD:]
    return probs, row_scale, (sums[:, :HD] * row_scale).astype(jnp.bfloat16)


def query_pair(block, part):
    first = block.shape[0] - 2
    return block[first, part], block[first + 1, part]


def scaled_grad(grad, row_scale, attended):
    grad = (grad.astype(jnp.float32) * row_scale).astype(jnp.bfloat16)
    products = attended.astype(jnp.float32) * grad.astype(jnp.float32)
    return grad, jnp.sum(products, axis=1, keepdims=True)


def backward_rows(query, grad, delta, probs, key_part, value_part):
    dprobs = lax.dot_general(grad, value_part, NT, preferred_element_type=jnp.float32)
    dscore = (probs.astype(jnp.float32) * (dprobs - delta)).astype(jnp.bfloat16)
    return (
        jnp.dot(dscore, key_part, preferred_element_type=jnp.float32),
        lax.dot_general(dscore, query, TN, preferred_element_type=jnp.float32),
        lax.dot_general(probs, grad, TN, preferred_element_type=jnp.float32),
    )


def forward_pass(query_blocks, outs, key_ref, value_ref, probs_ref, scale_ref):
    rows = outs[0].shape[1]
    step = min(FORWARD_ROWS, rows)
    key_all = key_ref[...]
    value_ones = value_ref[...]
    for index, block in enumerate(query_blocks):
        for start in range(0, rows, step):
            part = slice(start, start + step)
            here = slice(index * rows + start, index * rows + start + step)
            probs, row_scale, attended = forward_rows(
                query_pair(block, part)[0], key_all, value_ones
            )
            probs_ref[here] = probs
            scale_ref[here] = row_scale
            outs[index][0, part] = attended


def row_parts(query_blocks, rows):
    step = min(BACKWARD_ROWS, rows)
    for index in range(len(query_blocks)):
        for start in range(0, rows, step):
            first = index * rows + start
            yield index, slice(start, start + step), slice(first, first + step)


def add_terms(terms_ref, given_ref, dkey, dvalue):
    terms_ref[0] = dkey if given_ref is None else given_ref[0] + dkey
    terms_ref[1] = dvalue if given_ref is None else given_ref[1] + dvalue


def near_kernel(chips, near, *refs):
    pair_blocks, refs = refs[: 2 * chips], refs[2 * chips :]
    outs, query_outs, refs = refs[:near], refs[near : 2 * near], refs[2 * near :]
    own_ref, other_ref, key_ref, value_ref, probs_ref, scale_ref = refs
    query_blocks = pair_blocks[:near]
    rows = outs[0].shape[1]
    half = chips * rows
    load_keys(pair_blocks, key_ref, value_ref)
    forward_pass(query_blocks, outs, key_ref, value_ref, probs_ref, scale_ref)
    for index, part, here in row_parts(query_blocks, rows):
        query, grad = query_pair(query_blocks[index], part)
        grad, delta = scaled_grad(grad, scale_ref[here], outs[index][0, part])
        dquery, dkey, dvalue = backward_rows(
            query, grad, delta, probs_ref[here], key_ref[...], value_ref[:, :HD]
        )
        query_outs[index][0, part] = (dquery * SCORE_SCALE).astype(jnp.bfloat16)
        add_terms(own_ref, own_ref if here.start else None, dkey[:half], dvalue[:half])
        add_terms(other_ref, other_ref if here.start else None, dkey[half:], dvalue[half:])


def far_kernel(half, key_ref, value_ref, block_ref, given_ref, out, probs_out, scale_ref, query_terms, other_ref, probs_ref, terms_ref):
    forward_pass([block_ref], [out], key_ref, value_ref, probs_ref, scale_ref)
    probs_out[...] = probs_ref[:, :half]
    for index, part, here in row_parts([block_ref], out.shape[1]):
        query, grad = query_pair(block_ref, part)
        grad, delta = scaled_grad(grad, scale_ref[here], out[0, part])
        dquery, dkey, dvalue = backward_rows(
            query, grad, delta, probs_ref[here, half:], key_ref[half:], value_ref[half:, :HD]
        )
        query_terms[here] = dquery
        add_terms(terms_ref, terms_ref if here.start else given_ref, dkey, dvalue)
    last = other_ref.dtype == jnp.bfloat16
    other_ref[0] = (terms_ref[0] * (SCORE_SCALE if last else 1.0)).astype(other_ref.dtype)
    other_ref[1] = terms_ref[1].astype(other_ref.dtype)


def own_kernel(half, far, *refs):
    key_ref, value_ref, given_ref, refs = *refs[:3], refs[3:]
    query_blocks, attended, probs, scale, query_terms = (
        refs[at * far : (at + 1) * far] for at in range(5)
    )
    query_outs, own_ref = refs[5 * far : -1], refs[-1]
    for index, block_ref in enumerate(query_blocks):
        for _, part, here in row_parts([block_ref], attended[index].shape[1]):
            query, grad = query_pair(block_ref, part)
            grad, delta = scaled_grad(grad, scale[index][here], attended[index][0, part])
            dquery, dkey, dvalue = backward_rows(
                query, grad, delta, probs[index][here], key_ref[:half], value_ref[:half, :HD]
            )
            dquery = (dquery + query_terms[index][here]) * SCORE_SCALE
            query_outs[index][0, part] = dquery.astype(jnp.bfloat16)
            fresh = index == 0 and here.start == 0
            add_terms(own_ref, given_ref if fresh else own_ref, dkey, dvalue)
    own_ref[0] *= SCORE_SCALE


def call_vmem(kernel, name, operands, outs, scratch, products, limit):
    return pl.pallas_call(
        kernel,
        out_shape=[jax.ShapeDtypeStruct(shape, dtype) for shape, dtype in outs],
        in_specs=vmem_specs(len(operands)),
        out_specs=vmem_specs(len(outs)),
        scratch_shapes=[pltpu.VMEM(shape, dtype) for shape, dtype in scratch],
        compiler_params=pltpu.CompilerParams(vmem_limit_bytes=limit),
        cost_estimate=pl.CostEstimate(flops=2 * products, bytes_accessed=MIB, transcendentals=0),
        name=name,
    )(*operands)


def add_kernel(chips, own_ref, other_ref, *refs):
    query_blocks, attended, outs = refs[:chips], refs[chips : 2 * chips], refs[2 * chips :]
    rows = outs[0].shape[1]
    for index, out in enumerate(outs):
        part = slice(index * rows, (index + 1) * rows)
        total = own_ref[:, part] + other_ref[:, part].astype(jnp.float32)
        out[0] = attended[index][0]
        out[1] = query_blocks[index][0]
        out[2:4] = total.astype(jnp.bfloat16)


def to_chip(array, offset):
    return lax.ppermute(
        array, "seq", [(i, i ^ (2 * offset)) for i in range(lax.axis_size("seq"))]
    )


def to_core(array):
    return lax.ppermute(array, "seq", [(i, i ^ 1) for i in range(lax.axis_size("seq"))])


def after(array, other):
    return lax.optimization_barrier((array, other))[0]


def shards_one_level(query_rows, key_rows, value_rows, grad_output):
    bf16, f32 = jnp.bfloat16, jnp.float32
    chips = lax.axis_size("seq") // 2
    near = 2
    far = chips - near
    rows = query_rows.shape[0]
    half, keys = chips * rows, 2 * chips * rows
    chip = (lax.axis_index("seq") // 2).reshape(1)
    pairs = [key_rows, value_rows]
    queries = [query_rows, grad_output]
    wanted = [("keys", offset, pairs) for offset in range(2, chips)]
    wanted += [("keys", offset, pairs + queries) for offset in (1, 0)]
    wanted += [("queries", offset, queries) for offset in range(2, chips)]
    moved = {}
    for name, offset, arrays in wanted:
        packed = pack(chip, arrays, offset)
        chip = after(chip, packed)
        moved[name, offset] = to_chip(packed, offset) if offset else packed
    pair_blocks = [moved["keys", offset] for offset in range(chips)]
    query_blocks = [moved["queries", offset] for offset in range(near, chips)]
    swapped = [to_core(pair_blocks[0])]
    for offset in range(1, chips):
        value = pair_blocks[offset]
        swapped.append(to_core(after(value, swapped[0]) if offset in (1,) else value))
    all_blocks = pair_blocks + swapped
    block = ((1, rows, HD), bf16)
    terms = ((2, half, HD), f32)
    *outs, own, other, key_all, value_ones = call_vmem(
        functools.partial(near_kernel, chips, near),
        "near",
        all_blocks,
        [block] * (2 * near) + [terms, terms, ((keys, HD), bf16), ((keys, 2 * HD), bf16)],
        [((near * rows, keys), bf16), ((near * rows, HD), f32)],
        6 * near * rows * keys * HD,
        20 * MIB,
    )
    attended, query_grads = outs[:near], outs[near:]
    parts = []
    for index in range(far):
        last = index == far - 1
        *part, other = call_vmem(
            functools.partial(far_kernel, half),
            "far",
            [key_all, value_ones, query_blocks[index], other],
            [block, ((rows, half), bf16), ((rows, HD), f32), ((rows, HD), f32), ((2, half, HD), bf16 if last else f32)],
            [((rows, keys), bf16), ((2, half, HD), f32)],
            8 * rows * half * HD,
            16 * MIB,
        )
        parts.append(part)
    other = to_core(other)
    columns = [list(column) for column in zip(*parts)]
    attended = attended + columns[0]
    *outs, own = call_vmem(
        functools.partial(own_kernel, half, far),
        "own",
        [key_all, value_ones, own] + query_blocks + sum(columns, []),
        [block] * far + [terms],
        [],
        4 * far * rows * half * HD,
        16 * MIB,
    )
    query_grads = query_grads + outs
    outs = call_vmem(
        functools.partial(add_kernel, chips),
        "add_partials",
        [own, other] + query_grads + attended,
        [((4, rows, HD), bf16)] * chips,
        [],
        rows,
        8 * MIB,
    )
    order = list(range(2, chips)) + [1]
    returned = [outs[0]] + [to_chip(outs[offset], offset) for offset in order]
    layout = [(offset, (0, 1, 2, 3)) for offset in [0] + order]
    return tuple(unpack(chip, returned, layout, query_rows.shape[1]))


def shards(query_rows, key_rows, value_rows, grad_output, dilation_offsets):
    seq_width = lax.axis_size("seq")
    if (
        dilation_offsets.shape[0] == 1
        and query_rows.shape[0] * seq_width == SEG
        and query_rows.shape[1] // HD * 2 == seq_width
    ):
        return shards_one_level(query_rows, key_rows, value_rows, grad_output)
    return shards_levels(query_rows, key_rows, value_rows, grad_output, dilation_offsets)


def solution(mesh):
    in_specs = (
        P(("groups", "seq"), "head"),
        P(("groups", "seq"), "head"),
        P(("groups", "seq"), "head"),
        P(("groups", "seq"), "head"),
        P(None, "head"),
    )
    out_specs = (
        P(("groups", "seq"), "head"),
        P(("groups", "seq"), "head"),
        P(("groups", "seq"), "head"),
        P(("groups", "seq"), "head"),
    )
    return jax.shard_map(shards, mesh=mesh, in_specs=in_specs, out_specs=out_specs, check_vma=False)
```

```python
import functools

import jax
import jax.numpy as jnp
from jax import lax
from jax.experimental import pallas as pl
from jax.experimental.pallas import tpu as pltpu
from jax.sharding import PartitionSpec as P

HD = 128
SEG = 2048


def shortened(array):

    def short(part):
        return part.astype(jnp.bfloat16) if part.dtype == jnp.float32 else part

    return jax.tree.map(short, array)


def from_partner(array, axis, stride):
    return lax.ppermute(array, axis, [(i, i ^ 1 << stride) for i in range(lax.axis_size(axis))])


def pick_rows(values, row_mask):
    stride = row_mask.shape[0]
    shaped = values.reshape((values.shape[0] // stride, stride) + values.shape[1:])
    mask_wide = row_mask.reshape(row_mask.shape + (1,) * (values.ndim - 2))
    return jnp.sum(jnp.where(mask_wide, shaped, jnp.zeros((), values.dtype)), axis=1)


def place_rows(values, row_mask):
    stride = row_mask.shape[0]
    mask_wide = row_mask.reshape(row_mask.shape + (1,) * (values.ndim - 2))
    spread = jnp.where(mask_wide, values[:, None], jnp.zeros((), values.dtype))
    return spread.reshape((values.shape[0] * stride,) + values.shape[1:])


def upper_of(seq_index, bit_number):
    return seq_index // 2**bit_number % 2 == 1


def widen_apart(buffers, bit_totals, seq_index):
    widened = []
    for buffer, bit_total in zip(buffers, bit_totals):
        for bit_number in range(bit_total):
            partner = jax.tree.map(
                lambda part, own: part.astype(own.dtype),
                from_partner(shortened(buffer), "seq", bit_number),
                buffer,
            )
            upper_side = upper_of(seq_index, bit_number)
            buffer = jnp.where(
                upper_side,
                jnp.concatenate([partner, buffer], 0),
                jnp.concatenate([buffer, partner], 0),
            )
        widened.append(buffer)
    return widened


def narrow_apart(buffers, bit_totals, seq_index):
    narrowed = []
    for buffer, bit_total in zip(buffers, bit_totals):
        for bit_number in reversed(range(bit_total)):
            half_rows = buffer.shape[0] // 2
            lower_half = buffer[:half_rows]
            upper_half = buffer[half_rows:]
            upper_side = upper_of(seq_index, bit_number)
            outgoing = jnp.where(upper_side, lower_half, upper_half)
            kept_half = jnp.where(upper_side, upper_half, lower_half)
            buffer = kept_half + from_partner(outgoing, "seq", bit_number)
        narrowed.append(buffer)
    return narrowed


def split_keys(gathered, head_count):
    width = head_count * HD
    key_all = gathered[:, :width].reshape(-1, head_count, HD)
    value_all = gathered[:, width : 2 * width].reshape(-1, head_count, HD)
    return (key_all, value_all)


def forward_level(query_part, gathered, head_count):
    score_scale = HD ** (-0.5)
    key_all, value_all = split_keys(gathered, head_count)
    scores = (
        jnp.einsum("nhd,khd->hnk", query_part, key_all, preferred_element_type=jnp.float32)
        * score_scale
    )
    row_peak = jnp.max(scores, axis=2, keepdims=True)
    row_sums = jnp.sum(jnp.exp(scores - row_peak), axis=2, keepdims=True)
    level_lse = row_peak + jnp.log(row_sums)
    level_probs = jnp.exp(scores - level_lse).astype(jnp.bfloat16)
    partial_value = jnp.einsum(
        "hnk,khd->nhd", level_probs, value_all, preferred_element_type=jnp.float32
    )
    return (partial_value, jnp.transpose(level_lse[:, :, 0]))


def backward_level(query_part, grad_part, total_part, delta_part, gathered, head_count):
    score_scale = HD ** (-0.5)
    key_all, value_all = split_keys(gathered, head_count)
    scores = (
        jnp.einsum("nhd,khd->hnk", query_part, key_all, preferred_element_type=jnp.float32)
        * score_scale
    )
    glob = jnp.exp(scores - jnp.transpose(total_part)[:, :, None])
    glob_low = glob.astype(jnp.bfloat16)
    value_part = jnp.einsum("hnk,nhd->khd", glob_low, grad_part, preferred_element_type=jnp.float32)
    dprob = jnp.einsum("nhd,khd->hnk", grad_part, value_all, preferred_element_type=jnp.float32)
    dscore = (glob * (dprob - jnp.transpose(delta_part)[:, :, None])).astype(jnp.bfloat16)
    query_part_grad = (
        jnp.einsum("hnk,khd->nhd", dscore, key_all, preferred_element_type=jnp.float32)
        * score_scale
    )
    key_part = (
        jnp.einsum("hnk,nhd->khd", dscore, query_part, preferred_element_type=jnp.float32)
        * score_scale
    )
    key_count = key_part.shape[0]
    grad_term = jnp.concatenate(
        [key_part.reshape(key_count, -1), value_part.reshape(key_count, -1)], axis=1
    )
    return (query_part_grad, grad_term)


def shards_levels(query_rows, key_rows, value_rows, grad_output, dilation_offsets):
    row_count = query_rows.shape[0]
    head_count = query_rows.shape[1] // HD
    level_count = dilation_offsets.shape[0]
    seq_index = lax.axis_index("seq")
    seq_width = lax.axis_size("seq")
    query_three = query_rows.reshape(row_count, head_count, HD)
    key_three = key_rows.reshape(row_count, head_count, HD)
    value_three = value_rows.reshape(row_count, head_count, HD)
    grad_three = grad_output.reshape(row_count, head_count, HD)
    level_masks = []
    full_masks = []
    query_parts = []
    kept_pieces = []
    segment_bits = []
    for level_no in range(level_count):
        stride = 2**level_no
        row_mask = (
            lax.broadcasted_iota(jnp.int32, (stride, head_count), 0)
            == dilation_offsets[level_no][None, :]
        )
        full_mask = (
            lax.broadcasted_iota(jnp.int32, (row_count, head_count), 0) % stride
            == dilation_offsets[level_no][None, :]
        )
        level_masks.append(row_mask)
        full_masks.append(full_mask)
        query_parts.append(pick_rows(query_three, row_mask))
        key_three_part = pick_rows(key_three, row_mask)
        value_three_part = pick_rows(value_three, row_mask)
        piece = jnp.concatenate(
            [
                key_three_part.reshape(row_count // stride, -1),
                value_three_part.reshape(row_count // stride, -1),
            ],
            axis=1,
        )
        kept_pieces.append(piece)
        segment_bits.append(
            min((SEG * stride // row_count).bit_length() - 1, seq_width.bit_length() - 1)
        )
    paired = list(range(level_count - 1))
    paired_bits = [segment_bits[member] for member in paired]
    widened = widen_apart([kept_pieces[member] for member in paired], paired_bits, seq_index)
    gathered = list(kept_pieces)
    for member, buffer in zip(paired, widened):
        gathered[member] = buffer
    gathered[level_count - 1] = lax.all_gather(
        kept_pieces[level_count - 1], "seq", axis=0, tiled=True
    )
    out_parts = []
    lse_full = []
    for level_no in range(level_count):
        partial_value, level_lse = forward_level(
            query_parts[level_no], gathered[level_no], head_count
        )
        out_parts.append(place_rows(partial_value, level_masks[level_no]))
        lse_full.append(place_rows(level_lse, level_masks[level_no]))
    row_peak = lse_full[0]
    for level_no in range(1, level_count):
        row_peak = jnp.maximum(
            row_peak, jnp.where(full_masks[level_no], lse_full[level_no], lse_full[0])
        )
    exp_total = jnp.zeros((row_count, head_count), jnp.float32)
    for level_no in range(level_count):
        exp_total = exp_total + jnp.where(
            full_masks[level_no], jnp.exp(lse_full[level_no] - row_peak), jnp.float32(0.0)
        )
    total_lse = row_peak + jnp.log(exp_total)
    combined = jnp.zeros((row_count, head_count, HD), jnp.float32)
    for level_no in range(level_count):
        weight = jnp.exp(lse_full[level_no] - total_lse)
        combined = combined + jnp.where(
            full_masks[level_no][:, :, None],
            weight[:, :, None] * out_parts[level_no],
            jnp.float32(0.0),
        )
    attended = combined.astype(jnp.bfloat16)
    delta = jnp.sum(attended.astype(jnp.float32) * grad_three.astype(jnp.float32), axis=2)
    query_acc = jnp.zeros((row_count, head_count, HD), jnp.float32)
    grad_terms = []
    for level_no in range(level_count):
        row_mask = level_masks[level_no]
        grad_part = pick_rows(grad_three, row_mask)
        total_part = pick_rows(total_lse, row_mask)
        delta_part = pick_rows(delta, row_mask)
        query_part_grad, grad_term = backward_level(
            query_parts[level_no], grad_part, total_part, delta_part, gathered[level_no], head_count
        )
        query_acc = query_acc + place_rows(query_part_grad, row_mask)
        grad_terms.append(grad_term)
    narrowed = narrow_apart([grad_terms[member] for member in paired], paired_bits, seq_index)
    owned = list(grad_terms)
    for member, buffer in zip(paired, narrowed):
        owned[member] = buffer
    top_term = grad_terms[level_count - 1]
    owned[level_count - 1] = lax.psum_scatter(top_term, "seq", scatter_dimension=0, tiled=True)
    key_acc = jnp.zeros((row_count, head_count, HD), jnp.float32)
    value_acc = jnp.zeros((row_count, head_count, HD), jnp.float32)
    for level_no in range(level_count):
        own_rows = owned[level_no]
        key_own = own_rows[:, : head_count * HD].reshape(-1, head_count, HD)
        value_own = own_rows[:, head_count * HD :].reshape(-1, head_count, HD)
        key_acc = key_acc + place_rows(key_own, level_masks[level_no])
        value_acc = value_acc + place_rows(value_own, level_masks[level_no])
    flat = (row_count, head_count * HD)
    return (
        attended.reshape(flat),
        query_acc.astype(jnp.bfloat16).reshape(flat),
        key_acc.astype(jnp.bfloat16).reshape(flat),
        value_acc.astype(jnp.bfloat16).reshape(flat),
    )


NT = (((1,), (1,)), ((), ()))
TN = (((0,), (0,)), ((), ()))
MIB = 2**20
FORWARD_ROWS = 128
BACKWARD_ROWS = 256
SCORE_SCALE = HD ** (-0.5)
EXP_SCALE = SCORE_SCALE * 1.4426950408889634


def vmem_specs(count):
    return [pl.BlockSpec(memory_space=pltpu.VMEM)] * count


def any_specs(count):
    return [pl.BlockSpec(memory_space=pl.ANY)] * count


def head_columns(chip, offset):
    return pl.ds(pl.multiple_of((chip ^ offset) * HD, HD), HD)


def pack(chip, arrays, offset):
    start = (chip[0] ^ offset) * HD
    return jnp.stack([lax.dynamic_slice_in_dim(array, start, HD, axis=1) for array in arrays])


def unpack_kernel(layout, chip_ref, *refs):
    count = max(max(arrays) for _, arrays in layout) + 1
    blocks, outs, sems = refs[: len(layout)], refs[-1 - count : -1], refs[-1]
    chip = chip_ref[0]
    copies = []
    for at, (offset, arrays) in enumerate(layout):
        for place, index in enumerate(arrays):
            copies.append(
                pltpu.make_async_copy(
                    blocks[at].at[place],
                    outs[index].at[:, head_columns(chip, offset)],
                    sems.at[at, place],
                )
            )
    for copy in copies:
        copy.start()
    for copy in copies:
        copy.wait()


def unpack(chip, blocks, layout, width, into=()):
    count = max(max(arrays) for _, arrays in layout) + 1
    rows = blocks[0].shape[1]
    return pl.pallas_call(
        functools.partial(unpack_kernel, layout),
        out_shape=[jax.ShapeDtypeStruct((rows, width), blocks[0].dtype)] * count,
        in_specs=[pl.BlockSpec(memory_space=pltpu.SMEM)] + any_specs(len(blocks) + len(into)),
        out_specs=any_specs(count),
        input_output_aliases={1 + len(blocks) + at: at for at in range(len(into))},
        scratch_shapes=[pltpu.SemaphoreType.DMA((len(layout), count))],
        compiler_params=pltpu.CompilerParams(vmem_limit_bytes=MIB),
        name="unpack",
    )(chip, *blocks, *into)


def load_keys(blocks, key_ref, value_ref):
    rows = blocks[0].shape[1]
    for index, block in enumerate(blocks):
        key_ref[index * rows : (index + 1) * rows] = block[0]
        value_ref[index * rows : (index + 1) * rows, :HD] = block[1]
    if value_ref.shape[1] > HD:
        value_ref[:, HD:] = jnp.ones((value_ref.shape[0], HD), value_ref.dtype)


def forward_rows(query, key_all, value_ones):
    scores = lax.dot_general(query, key_all, NT, preferred_element_type=jnp.float32)
    row_peak = jnp.max(scores, axis=1, keepdims=True)
    probs = jnp.exp2(scores * EXP_SCALE - row_peak * EXP_SCALE).astype(jnp.bfloat16)
    sums = jnp.dot(probs, value_ones, preferred_element_type=jnp.float32)
    row_scale = 1.0 / sums[:, HD:]
    return probs, row_scale, (sums[:, :HD] * row_scale).astype(jnp.bfloat16)


def query_pair(block, part):
    first = block.shape[0] - 2
    return block[first, part], block[first + 1, part]


def scaled_grad(grad, row_scale, attended):
    grad = (grad.astype(jnp.float32) * row_scale).astype(jnp.bfloat16)
    products = attended.astype(jnp.float32) * grad.astype(jnp.float32)
    return grad, jnp.sum(products, axis=1, keepdims=True)


def backward_rows(query, grad, delta, probs, key_part, value_part):
    dprobs = lax.dot_general(grad, value_part, NT, preferred_element_type=jnp.float32)
    dscore = (probs.astype(jnp.float32) * (dprobs - delta)).astype(jnp.bfloat16)
    return (
        jnp.dot(dscore, key_part, preferred_element_type=jnp.float32),
        lax.dot_general(dscore, query, TN, preferred_element_type=jnp.float32),
        lax.dot_general(probs, grad, TN, preferred_element_type=jnp.float32),
    )


def forward_pass(query_blocks, outs, key_ref, value_ref, probs_ref, scale_ref):
    rows = outs[0].shape[1]
    step = min(FORWARD_ROWS, rows)
    key_all = key_ref[...]
    value_ones = value_ref[...]
    for index, block in enumerate(query_blocks):
        for start in range(0, rows, step):
            part = slice(start, start + step)
            here = slice(index * rows + start, index * rows + start + step)
            probs, row_scale, attended = forward_rows(
                query_pair(block, part)[0], key_all, value_ones
            )
            probs_ref[here] = probs
            scale_ref[here] = row_scale
            outs[index][0, part] = attended


def row_parts(query_blocks, rows):
    step = min(BACKWARD_ROWS, rows)
    for index in range(len(query_blocks)):
        for start in range(0, rows, step):
            first = index * rows + start
            yield index, slice(start, start + step), slice(first, first + step)


def add_terms(terms_ref, given_ref, dkey, dvalue):
    terms_ref[0] = dkey if given_ref is None else given_ref[0] + dkey
    terms_ref[1] = dvalue if given_ref is None else given_ref[1] + dvalue


def near_kernel(chips, near, *refs):
    pair_blocks, refs = refs[: 2 * chips], refs[2 * chips :]
    outs, query_outs, refs = refs[:near], refs[near : 2 * near], refs[2 * near :]
    own_ref, other_ref, key_ref, value_ref, probs_ref, scale_ref = refs
    query_blocks = pair_blocks[:near]
    rows = outs[0].shape[1]
    half = chips * rows
    load_keys(pair_blocks, key_ref, value_ref)
    forward_pass(query_blocks, outs, key_ref, value_ref, probs_ref, scale_ref)
    for index, part, here in row_parts(query_blocks, rows):
        query, grad = query_pair(query_blocks[index], part)
        grad, delta = scaled_grad(grad, scale_ref[here], outs[index][0, part])
        dquery, dkey, dvalue = backward_rows(
            query, grad, delta, probs_ref[here], key_ref[...], value_ref[:, :HD]
        )
        query_outs[index][0, part] = (dquery * SCORE_SCALE).astype(jnp.bfloat16)
        add_terms(own_ref, own_ref if here.start else None, dkey[:half], dvalue[:half])
        add_terms(other_ref, other_ref if here.start else None, dkey[half:], dvalue[half:])


def far_kernel(half, key_ref, value_ref, block_ref, given_ref, out, probs_out, scale_ref, query_terms, other_ref, probs_ref, terms_ref):
    forward_pass([block_ref], [out], key_ref, value_ref, probs_ref, scale_ref)
    probs_out[...] = probs_ref[:, :half]
    for index, part, here in row_parts([block_ref], out.shape[1]):
        query, grad = query_pair(block_ref, part)
        grad, delta = scaled_grad(grad, scale_ref[here], out[0, part])
        dquery, dkey, dvalue = backward_rows(
            query, grad, delta, probs_ref[here, half:], key_ref[half:], value_ref[half:, :HD]
        )
        query_terms[here] = dquery
        add_terms(terms_ref, terms_ref if here.start else given_ref, dkey, dvalue)
    last = other_ref.dtype == jnp.bfloat16
    other_ref[0] = (terms_ref[0] * (SCORE_SCALE if last else 1.0)).astype(other_ref.dtype)
    other_ref[1] = terms_ref[1].astype(other_ref.dtype)


def own_kernel(half, far, *refs):
    key_ref, value_ref, given_ref, refs = *refs[:3], refs[3:]
    query_blocks, attended, probs, scale, query_terms = (
        refs[at * far : (at + 1) * far] for at in range(5)
    )
    query_outs, own_ref = refs[5 * far : -1], refs[-1]
    for index, block_ref in enumerate(query_blocks):
        for _, part, here in row_parts([block_ref], attended[index].shape[1]):
            query, grad = query_pair(block_ref, part)
            grad, delta = scaled_grad(grad, scale[index][here], attended[index][0, part])
            dquery, dkey, dvalue = backward_rows(
                query, grad, delta, probs[index][here], key_ref[:half], value_ref[:half, :HD]
            )
            dquery = (dquery + query_terms[index][here]) * SCORE_SCALE
            query_outs[index][0, part] = dquery.astype(jnp.bfloat16)
            fresh = index == 0 and here.start == 0
            add_terms(own_ref, given_ref if fresh else own_ref, dkey, dvalue)
    own_ref[0] *= SCORE_SCALE


def call_vmem(kernel, name, operands, outs, scratch, products, limit):
    return pl.pallas_call(
        kernel,
        out_shape=[jax.ShapeDtypeStruct(shape, dtype) for shape, dtype in outs],
        in_specs=vmem_specs(len(operands)),
        out_specs=vmem_specs(len(outs)),
        scratch_shapes=[pltpu.VMEM(shape, dtype) for shape, dtype in scratch],
        compiler_params=pltpu.CompilerParams(vmem_limit_bytes=limit),
        cost_estimate=pl.CostEstimate(flops=2 * products, bytes_accessed=MIB, transcendentals=0),
        name=name,
    )(*operands)


def add_kernel(chips, own_ref, other_ref, *refs):
    query_blocks, attended, outs = refs[:chips], refs[chips : 2 * chips], refs[2 * chips :]
    rows = outs[0].shape[1]
    for index, out in enumerate(outs):
        part = slice(index * rows, (index + 1) * rows)
        total = own_ref[:, part] + other_ref[:, part].astype(jnp.float32)
        out[0] = attended[index][0]
        out[1] = query_blocks[index][0]
        out[2:4] = total.astype(jnp.bfloat16)


def to_chip(array, offset):
    return lax.ppermute(
        array, "seq", [(i, i ^ (2 * offset)) for i in range(lax.axis_size("seq"))]
    )


def to_core(array):
    return lax.ppermute(array, "seq", [(i, i ^ 1) for i in range(lax.axis_size("seq"))])


def after(array, other):
    return lax.optimization_barrier((array, other))[0]


def shards_one_level(query_rows, key_rows, value_rows, grad_output):
    bf16, f32 = jnp.bfloat16, jnp.float32
    chips = lax.axis_size("seq") // 2
    near = 2
    far = chips - near
    rows = query_rows.shape[0]
    half, keys = chips * rows, 2 * chips * rows
    chip = (lax.axis_index("seq") // 2).reshape(1)
    pairs = [key_rows, value_rows]
    queries = [query_rows, grad_output]
    wanted = [("keys", 2, pairs), ("keys", 1, pairs + queries)]
    wanted += [("keys", offset, pairs) for offset in range(3, chips)]
    wanted += [("keys", 0, pairs + queries)]
    wanted += [("queries", offset, queries) for offset in range(2, chips)]
    moved = {}
    for name, offset, arrays in wanted:
        packed = pack(chip, arrays, offset)
        chip = after(chip, packed)
        moved[name, offset] = to_chip(packed, offset) if offset else packed
    pair_blocks = [moved["keys", offset] for offset in range(chips)]
    query_blocks = [moved["queries", offset] for offset in range(near, chips)]
    swapped = [to_core(pair_blocks[0])]
    for offset in range(1, chips):
        value = pair_blocks[offset]
        swapped.append(to_core(after(value, swapped[0]) if offset in (1,) else value))
    all_blocks = pair_blocks + swapped
    block = ((1, rows, HD), bf16)
    terms = ((2, half, HD), f32)
    *outs, own, other, key_all, value_ones = call_vmem(
        functools.partial(near_kernel, chips, near),
        "near",
        all_blocks,
        [block] * (2 * near) + [terms, terms, ((keys, HD), bf16), ((keys, 2 * HD), bf16)],
        [((near * rows, keys), bf16), ((near * rows, HD), f32)],
        6 * near * rows * keys * HD,
        20 * MIB,
    )
    attended, query_grads = outs[:near], outs[near:]
    parts = []
    for index in range(far):
        last = index == far - 1
        *part, other = call_vmem(
            functools.partial(far_kernel, half),
            "far",
            [key_all, value_ones, query_blocks[index], other],
            [block, ((rows, half), bf16), ((rows, HD), f32), ((rows, HD), f32), ((2, half, HD), bf16 if last else f32)],
            [((rows, keys), bf16), ((2, half, HD), f32)],
            8 * rows * half * HD,
            16 * MIB,
        )
        parts.append(part)
    other = to_core(other)
    columns = [list(column) for column in zip(*parts)]
    attended = attended + columns[0]
    *outs, own = call_vmem(
        functools.partial(own_kernel, half, far),
        "own",
        [key_all, value_ones, own] + query_blocks + sum(columns, []),
        [block] * far + [terms],
        [],
        4 * far * rows * half * HD,
        16 * MIB,
    )
    query_grads = query_grads + outs
    outs = call_vmem(
        functools.partial(add_kernel, chips),
        "add_partials",
        [own, other] + query_grads + attended,
        [((4, rows, HD), bf16)] * chips,
        [],
        rows,
        8 * MIB,
    )
    order = [2, 1] + list(range(3, chips))
    returned = [outs[0]] + [to_chip(outs[offset], offset) for offset in order]
    layout = [(offset, (0, 1, 2, 3)) for offset in [0] + order]
    width = query_rows.shape[1]
    last = layout.index((chips - 1, (0, 1, 2, 3)))
    returned.append(returned.pop(last))
    layout.append(layout.pop(last))
    arrays = unpack(chip, returned[:-1], layout[:-1], width)
    return tuple(unpack(chip, returned[-1:], layout[-1:], width, arrays))


def shards(query_rows, key_rows, value_rows, grad_output, dilation_offsets):
    seq_width = lax.axis_size("seq")
    if (
        dilation_offsets.shape[0] == 1
        and query_rows.shape[0] * seq_width == SEG
        and query_rows.shape[1] // HD * 2 == seq_width
    ):
        return shards_one_level(query_rows, key_rows, value_rows, grad_output)
    return shards_levels(query_rows, key_rows, value_rows, grad_output, dilation_offsets)


def solution(mesh):
    in_specs = (
        P(("groups", "seq"), "head"),
        P(("groups", "seq"), "head"),
        P(("groups", "seq"), "head"),
        P(("groups", "seq"), "head"),
        P(None, "head"),
    )
    out_specs = (
        P(("groups", "seq"), "head"),
        P(("groups", "seq"), "head"),
        P(("groups", "seq"), "head"),
        P(("groups", "seq"), "head"),
    )
    return jax.shard_map(shards, mesh=mesh, in_specs=in_specs, out_specs=out_specs, check_vma=False)
```
